1024 devices in a mesh: dp: 16 (over z_lo), node: 4 (over z_hi, core), innode: 16 (over y, x).
Axes of the slice: x: 4, y: 4, z: 32 (z_hi: 2, z_lo: 16; z = z_hi * 16 + z_lo), core: 2. Of those that a mesh axis runs over, the one named last changes fastest.
Arguments:
- tokens: bfloat16 [64, 16, 4096], P(('node', 'innode'), 'dp'), may hold values from -6 to 6
- routes: int32 [64, 16, 8], P(('node', 'innode'), 'dp'), may hold values from 0 to 63, all different within a row; in each aligned block of 16 rows (0 to 15, 16 to 31, ..., all dimensions but the last counted through in order) at most 4 rows name the same one
- gate_num: int32 [64, 16, 8], P(('node', 'innode'), 'dp'), may hold values from 16 to 128
- w_gate: bfloat16 [64, 4096, 2048], P(('node', 'innode'), None, 'dp'), may hold values from -0.09375 to 0.09375
- w_up: bfloat16 [64, 4096, 2048], P(('node', 'innode'), None, 'dp'), may hold values from -0.09375 to 0.09375
- w_down: bfloat16 [64, 2048, 4096], P(('node', 'innode'), 'dp'), may hold values from -0.125 to 0.125
Outputs:
- combined: bfloat16 [64, 16, 4096], P(('node', 'innode'), 'dp')
- expert_load: float32 [64], replicated
- balance_loss: float32 [], replicated
The draws below stay inside these ranges and needn't reach their ends.
Inputs may be any that keep to these rules, and one draw needn't show every extreme that they name: `routes`: each token names 8 different experts and every expert is named somewhere. Within each aligned block of 16 tokens (one column, one index of node and innode) no expert is named by more than 4 tokens, and in some blocks some expert is named by exactly 4. `gate_num`: gate weight numerators over 256.
All inputs are finite; a program needn't handle non-finite values.
Results may differ from the reference program's by a relative error of at most 0.008.
Values may be sent and summed in bfloat16 or wider, within the bound.
A program may use at most 32 MiB of HBM per device.

```python
import math
import jax
import jax.numpy as jnp
import numpy as np
from jax import lax

D = 4096
HIDDEN_SIZE = 2048
GATE_DEN = 256
COLS = 64
COL_TOK = 16
TOKENS = 1024
EXPERTS = 64
TOPK = 8
CAP = 4
N_DP = 16


def touch_ends(values, rng, least, high):
    place = [jax.random.randint(jax.random.fold_in(rng, axis), (), 0, length) for axis, length in enumerate(values.shape)]
    widest = values.shape.index(max(values.shape))
    beside = place[:widest] + [(place[widest] + 1) % values.shape[widest]] + place[widest + 1:]
    return values.at[tuple(place)].set(least).at[tuple(beside)].set(high)


def block_levels(key, shape, cuts, smallest, top_value):
    gain = 1.0
    for dim, blocks in cuts:
        heights = jax.random.uniform(jax.random.fold_in(jax.random.fold_in(key, 6), dim), (blocks,), jnp.float32, smallest / len(cuts), top_value / len(cuts))
        gain = gain * jnp.repeat(jnp.exp(heights), shape[dim] // blocks).reshape((-1,) + (1,) * (len(shape) - 1 - dim))
    return gain


def deal_out(stream_key, own, number, rows, number_of, top, bound, lean):
    sequence = jax.random.permutation(stream_key, number_of)
    heavy_load, ordinary = load_shares(number_of, rows * top, bound, lean, True), load_shares(number_of, rows * top, bound, lean, False)
    places = jnp.arange(number_of)

    def named(lengths, offset_by):
        used = int((lengths > 0).sum())
        fixed = max(1, used // 4)
        moved = fixed + (places - fixed + offset_by * (used - fixed)) % max(1, number_of - fixed)
        return jnp.zeros((number_of,), jnp.int32).at[sequence[jnp.where(places < fixed, places, moved)]].set(jnp.asarray(lengths, jnp.int32))

    lengths = jnp.where(number % 4 == 0, named(heavy_load, number // 4), named(ordinary, number - number // 4 - 1))
    mixed = jax.random.permutation(jax.random.fold_in(own, 3), number_of)
    source_of, taker = mixed[0:number_of // 2 * 2:2], mixed[1:number_of // 2 * 2:2]
    margin = jnp.minimum(lengths[source_of] - 1, bound - lengths[taker]) // 2
    margin = jnp.where((source_of == sequence[0]) | (taker == sequence[0]) | (lengths[taker] == 0), 0, jnp.maximum(margin, 0))
    moved = jax.random.randint(jax.random.fold_in(own, 4), (number_of // 2,), 0, 1 << 20) % (margin + 1)
    lengths = lengths.at[source_of].add(-moved).at[taker].add(moved)
    items = jnp.searchsorted(jnp.cumsum(lengths), jnp.arange(rows * top), side="right").astype(jnp.int32)
    grid = items.reshape(top, rows).T
    grid = grid[jax.random.permutation(jax.random.fold_in(own, 1), rows)]
    offset_by = jax.random.randint(jax.random.fold_in(own, 2), (rows, 1), 0, top)
    return jnp.take_along_axis(grid, (jnp.arange(top)[None, :] + offset_by) % top, axis=1)


def load_shares(amount, total, reach, lean, full):
    weights = [(1 << 20) // math.isqrt(grade ** lean) + 1 for grade in range(1, amount + 1)]
    largest = reach if full else min(reach, max(-(-total // amount), total * weights[0] // sum(weights)))
    least = 1 if total - largest >= amount - 1 else 0
    given, surplus = [largest] + [least] * (amount - 1), total - largest - least * (amount - 1)
    while surplus > 0:
        free = [i for i in range(1, amount) if given[i] < largest] or [i for i in range(1, amount) if given[i] < reach]
        mass, remaining = sum([weights[i] for i in free]), surplus
        for i in free:
            more = min(reach - given[i], max(1, remaining * weights[i] // mass), surplus)
            given[i] = given[i] + more
            surplus = surplus - more
    return np.array(given)


def normal_values(rng, extent, spread, bound, cuts=(), kind=jnp.bfloat16):
    result = spread * jax.random.normal(rng, extent, jnp.float32)
    if cuts:
        result = result * block_levels(rng, extent, cuts, -0.22, 0.18)
    return jnp.clip(result, -bound, bound).astype(kind)


def setup_inputs(seed: int = 0) -> dict:
    splits = jax.random.split(jax.random.key(seed), 7)
    tokens = normal_values(splits[0], (COLS, COL_TOK, D), 1.0, 6.0, ((0, 64), (1, 16)))
    routes_keys = jax.random.split(jax.random.fold_in(splits[1], 1), COLS * COL_TOK // COL_TOK)
    routes_turns = jax.random.permutation(jax.random.fold_in(splits[1], 3), COLS * COL_TOK // COL_TOK)
    routes = jax.vmap(lambda own, number: deal_out(jax.random.fold_in(splits[1], 2), own, number, COL_TOK, EXPERTS, TOPK, CAP, 2))(routes_keys, routes_turns).reshape((COLS, COL_TOK, TOPK))
    gate_num = touch_ends(jax.random.randint(splits[2], (COLS, COL_TOK, TOPK), 16, 129), jax.random.fold_in(splits[2], 1), 16, 128).astype(jnp.int32)
    w_gate = normal_values(splits[3], (EXPERTS, D, HIDDEN_SIZE), D ** -0.5, 0.09375, ((0, 64), (2, 16)))
    w_up = normal_values(splits[4], (EXPERTS, D, HIDDEN_SIZE), D ** -0.5, 0.09375, ((0, 64), (2, 16)))
    w_down = normal_values(splits[5], (EXPERTS, HIDDEN_SIZE, D), HIDDEN_SIZE ** -0.5, 0.125, ((0, 64), (1, 16)))
    return {"tokens": tokens, "routes": routes, "gate_num": gate_num, "w_gate": w_gate, "w_up": w_up, "w_down": w_down}


def column_ranks(column_routes):
    flat_routes = column_routes.reshape(-1)
    onehot = (flat_routes[:, None] == jnp.arange(EXPERTS, dtype=jnp.int32)[None, :]).astype(jnp.int32)
    before = (jnp.cumsum(onehot, axis=0) - onehot).astype(jnp.int32)
    position = jnp.sum(before * onehot, axis=1).astype(jnp.int32)
    return position.reshape(column_routes.shape)


def one_expert(operands):
    row_block, gate_w, up_w, down_w = operands
    gate_proj = jnp.dot(row_block, gate_w, preferred_element_type=jnp.float32)
    up_proj = jnp.dot(row_block, up_w, preferred_element_type=jnp.float32)
    hidden = (jax.nn.silu(gate_proj) * up_proj).astype(jnp.bfloat16)
    blocks = hidden.reshape(-1, N_DP, HIDDEN_SIZE // N_DP).astype(jnp.float32)
    down_blocks = down_w.reshape(N_DP, HIDDEN_SIZE // N_DP, D).astype(jnp.float32)
    pieces = jnp.einsum("rsh,shd->rsd", blocks, down_blocks)
    pieces = lax.optimization_barrier(pieces.astype(jnp.bfloat16))
    return jnp.sum(pieces.astype(jnp.float32), axis=1)


def reference(tokens, routes, gate_num, w_gate, w_up, w_down):
    position = jax.vmap(column_ranks)(routes)
    column_ids = jnp.arange(COLS, dtype=jnp.int32)[:, None, None]
    placed = (column_ids * CAP + position).astype(jnp.int32)
    spread_rows = jnp.broadcast_to(tokens[:, :, None, :], (COLS, COL_TOK, TOPK, D))
    buckets = jnp.zeros((EXPERTS, COLS * CAP, D), jnp.bfloat16).at[routes, placed].set(spread_rows)
    outputs = lax.map(one_expert, (buckets, w_gate, w_up, w_down))
    picked = outputs[routes, placed]
    weights = gate_num.astype(jnp.float32) / GATE_DEN
    combined = jnp.einsum("ctk,ctkd->ctd", weights, picked).astype(jnp.bfloat16)
    matches = (routes[..., None] == jnp.arange(EXPERTS, dtype=jnp.int32)).astype(jnp.float32)
    counts = jnp.sum(matches, axis=(0, 1, 2))
    expert_load = counts * (EXPERTS / (TOPK * TOKENS))
    numerators = gate_num.astype(jnp.float32)
    shares = numerators / jnp.sum(numerators, axis=-1, keepdims=True)
    mean_share = jnp.einsum("ctk,ctke->e", shares, matches) / TOKENS
    balance_loss = jnp.sum(expert_load * mean_share)
    return combined, expert_load, balance_loss
```

```python
import functools

import jax
import jax.numpy as jnp
from jax import lax
from jax.experimental import pallas as pl
from jax.experimental.pallas import tpu as pltpu
from jax.sharding import PartitionSpec as P

GATE_DEN = 256
MESH = pl.DeviceIdType.MESH
SIDE = 4
FAR = 4


def kernel(
    dims,
    tok,
    meta,
    wg,
    wu,
    wd,
    out,
    stats,
    x3,
    mz,
    codes,
    spread,
    meta_t,
    xb,
    w1,
    w2,
    pa,
    ps,
    pr,
    h_own,
    h_oth,
    gates_t,
    ob,
    rh,
    rf,
    y3,
    rn,
    ya,
    rz,
    ssem,
    rsem,
    lsem,
):
    n_dp, feats, experts, per_token, total_tokens = dims
    ring = 2 * n_dp
    near = ring // FAR
    chunk = ring
    half = chunk // 2
    tiles = feats // 256
    part = feats // 4
    hid = wd.shape[1]
    f32, bf16 = jnp.float32, jnp.bfloat16

    dp = lax.axis_index("dp")
    node = lax.axis_index("node")
    inn = lax.axis_index("innode")
    z = lax.div(node, 2) * n_dp + dp
    core = lax.rem(node, 2)
    other = 1 - core
    py = lax.div(inn, SIDE)
    px = lax.rem(inn, SIDE)
    r = lax.rem(z, near)
    j = lax.div(z, near)

    def device(zz, cc, yy, xx):
        return (lax.rem(zz, n_dp), lax.div(zz, n_dp) * 2 + cc, yy * SIDE + xx)

    def ringz(o):
        return lax.rem(z + (o + ring), ring)

    def side(p, o):
        return lax.rem(p + (o + SIDE), SIDE)

    def slot(jj, cc):
        return lax.div(jj, 2) * chunk + r * 4 + lax.rem(jj, 2) * 2 + cc

    near_offsets = [o for o in range(-(near // 2 - 1) if near > 1 else 0, near // 2 + 1) if o != 0]
    far_steps = [(dj, dc) for dj in range(FAR) for dc in range(2) if (dj, dc) != (0, 0)]

    def far_device(dj, dc):
        jj = lax.rem(j + dj, FAR)
        cc = lax.rem(core + dc, 2)
        return jj, cc, device(r + near * jj, cc, py, px)

    barrier = pltpu.get_barrier_semaphore()
    greet = [far_device(dj, dc)[2] for dj, dc in far_steps]
    greet += [device(ringz(-o), core, py, px) for o in near_offsets]
    greet += [device(z, core, py, side(px, o)) for o in (1, 2, -1)]
    greet += [device(z, core, side(py, o), px) for o in (1, 2, -1)]
    for target in greet:
        pl.semaphore_signal(barrier, inc=1, device_id=target, device_id_type=MESH)

    local = []

    def load(src, dst):
        copy = pltpu.make_async_copy(src, dst, lsem.at[len(local)])
        copy.start()
        local.append(copy)

    def rows_of(c, h):
        return pl.ds(pl.multiple_of(c * (2 * part) + h * part, part), part)

    for h in range(2):
        load(wg.at[0, rows_of(core, h), :], w1.at[h, :, pl.ds(0, hid)])
        load(wu.at[0, rows_of(core, h), :], w1.at[h, :, pl.ds(hid, hid)])
    lanes_own = pl.ds(pl.multiple_of(core * (2 * part), 2 * part), 2 * part)
    lanes_oth = pl.ds(pl.multiple_of(other * (2 * part), 2 * part), 2 * part)
    load(wd.at[0, :, lanes_own], w2.at[pl.ds(0, hid), :])

    x3[slot(j, core)] = tok[core]
    mz[lax.div(j, 2), r * 4 + lax.rem(j, 2) * 2 + core] = meta[...]

    pl.semaphore_wait(barrier, len(greet))

    sent = {}

    def send(key, src, dst, target):
        i = len(sent)
        copy = pltpu.make_async_remote_copy(
            src_ref=src,
            dst_ref=dst,
            send_sem=ssem.at[i],
            recv_sem=rsem.at[i],
            device_id=target,
            device_id_type=MESH,
        )
        copy.start()
        sent[key] = copy

    def recv(key):
        sent[key].wait_recv()

    partner = device(z, other, py, px)

    own_slot = slot(j, core)
    own_meta = (lax.div(j, 2), r * 4 + lax.rem(j, 2) * 2 + core)
    for dj, dc in far_steps:
        jj, cc, target = far_device(dj, dc)
        send(("far", dj, dc), tok.at[cc], x3.at[own_slot], target)
    for dj, dc in far_steps:
        jj, cc, target = far_device(dj, dc)
        send(("farm", dj, dc), meta, mz.at[own_meta], target)

    for h in range(2):
        send(("wg", h), wg.at[0, rows_of(other, h), :], w1.at[h, :, pl.ds(2 * hid, hid)], partner)
        send(("wu", h), wu.at[0, rows_of(other, h), :], w1.at[h, :, pl.ds(3 * hid, hid)], partner)
    send(("wd",), wd.at[0, :, lanes_oth], w2.at[pl.ds(hid, hid), :], partner)

    for dj, dc in far_steps:
        recv(("far", dj, dc))
    for q in range(2):
        group = x3.at[pl.ds(q * chunk + r * 4, 4)]
        for o in near_offsets:
            send(("near", q, o), group, group, device(ringz(o), core, py, px))
        if q == 0:
            for dj, dc in far_steps:
                recv(("farm", dj, dc))
            group = mz.at[:, pl.ds(r * 4, 4)]
            for o in near_offsets:
                send(("nearm", o), group, group, device(ringz(o), core, py, px))

    def place(h, da, db):
        return (side(py, db), side(px, da)) if h == 0 else (side(py, da), side(px, db))

    def xy_device(h, da, db):
        yy, xx = place(h, da, db)
        return device(z, core, yy, xx)

    def block(ref, q, h, da, db, rows=None):
        yy, xx = place(h, da, db)
        return ref.at[q, h, yy, xx] if rows is None else ref.at[q, h, yy, xx, rows]

    low, high = pl.ds(0, half), pl.ds(half, half)

    def ag_own(q):
        for d in (1, -1):
            for h in range(2):
                src = block(xb, q, h, 0, 0)
                send(("p1", q, h, d), src, src, xy_device(h, d, 0))
        for h in range(2):
            ag_second(q, h, 0)

    def ag_second(q, h, a):
        src = block(xb, q, h, a, 0)
        for d in (1, -1):
            send(("p2", q, h, a, d), src, src, xy_device(h, 0, d))

    def ag_first_forward(q):
        for d in (1, -1):
            for h in range(2):
                recv(("p1", q, h, d))
                src = block(xb, q, h, -d, 0, low if d == 1 else high)
                send(("p1f", q, h, d), src, src, xy_device(h, d, 0))
                ag_second(q, h, -d)

    def ag_second_forward(q, a):
        for h in range(2):
            for d in (1, -1):
                recv(("p2", q, h, a, d))
                src = block(xb, q, h, a, -d, low if d == 1 else high)
                send(("p2f", q, h, a, d), src, src, xy_device(h, 0, d))

    def ag_opposite(q):
        for h in range(2):
            for d in (1, -1):
                recv(("p1f", q, h, d))
            ag_second(q, h, 2)

    def ag_finish(q):
        for a in (0, 1, -1, 2):
            for h in range(2):
                for d in (1, -1):
                    recv(("p2f", q, h, a, d))

    def spread_in(q):
        for o in near_offsets:
            recv(("near", q, o))
        spread[...] = x3[pl.ds(q * chunk, chunk)].astype(f32)
        per = part // 128
        for h in range(2):
            for i in range(per):
                xb[q, h, py, px, :, pl.ds(i * 128, 128)] = spread[:, h * per + i, :].astype(bf16)

    spread_in(0)
    ag_own(0)

    for o in near_offsets:
        recv(("nearm", o))
    meta_t[...] = jnp.full_like(meta_t, -1.0)
    for q in range(2):
        meta_t[pl.ds(q * chunk, chunk), :] = mz[q, :, 0, :]
    codes[py, px] = jnp.transpose(meta_t[...])[0 : 2 * per_token]
    for o in (1, -1, 2):
        src = codes.at[py, px]
        send(("mx", o), src, src, device(z, core, py, side(px, o)))

    ag_first_forward(0)
    spread_in(1)
    ag_second_forward(0, 0)
    for o in (1, -1, 2):
        recv(("mx", o))
    for o in (1, -1, 2):
        src = codes.at[py]
        send(("my", o), src, src, device(z, core, side(py, o), px))
    ag_opposite(0)
    ag_own(1)
    ag_second_forward(0, 1)
    ag_second_forward(0, -1)
    ag_first_forward(1)
    ag_second_forward(0, 2)
    ag_second_forward(1, 0)
    ag_opposite(1)

    for o in (1, -1, 2):
        recv(("my", o))
    expert = (node * (SIDE * SIDE) + inn).astype(f32)
    rows_e = lax.broadcasted_iota(jnp.int32, (experts, 128), 0).astype(f32)
    counts = jnp.zeros((experts, 128), f32)
    share_sums = jnp.zeros((experts, 128), f32)
    meta_t[...] = jnp.zeros_like(meta_t)
    for yy in range(SIDE):
        for xx in range(SIDE):
            table = codes[yy, xx]
            route, numer = table[0:per_token], table[per_token : 2 * per_token]
            valid = route >= 0
            numer = jnp.where(valid, numer, 0.0)
            total = jnp.sum(numer, axis=0, keepdims=True)
            share = numer / jnp.where(total > 0, total, 1.0)
            meta_t[pl.ds(yy * SIDE + xx, 1), :] = jnp.sum(
                jnp.where(route == expert, numer, 0.0), axis=0, keepdims=True
            ) * (1.0 / GATE_DEN)
            for k in range(per_token):
                hit = rows_e == route[k : k + 1]
                counts = counts + jnp.where(hit, 1.0, 0.0)
                share_sums = share_sums + jnp.where(hit, share[k : k + 1], 0.0)
    gates_t[...] = jnp.transpose(meta_t[...])
    load_col = jnp.sum(counts, axis=1, keepdims=True) * (experts / (per_token * total_tokens))
    mean_col = jnp.sum(share_sums, axis=1, keepdims=True) / total_tokens
    meta_t[pl.ds(0, experts), :] = jnp.broadcast_to(load_col, (experts, 128))
    stats[pl.ds(0, 1), :] = jnp.transpose(meta_t[...])[0:1]
    stats[pl.ds(1, 1), :] = jnp.broadcast_to(jnp.sum(load_col * mean_col, axis=0, keepdims=True), (1, 128))

    for copy in local:
        copy.wait()
    for h in range(2):
        recv(("wg", h))
        recv(("wu", h))
    recv(("wd",))

    rows = SIDE * chunk

    def project(q):
        def body(yy, carry):
            acc = jnp.dot(xb[q, 0, yy].reshape(rows, part), w1[0], preferred_element_type=f32)
            acc = acc + jnp.dot(xb[q, 1, yy].reshape(rows, part), w1[1], preferred_element_type=f32)
            pa[q, yy] = acc[:, 0 : 2 * hid]
            ps[q, yy] = acc[:, 2 * hid : 4 * hid]
            return carry

        lax.fori_loop(0, SIDE, body, 0)
        send(("ps", q), ps.at[q], pr.at[q], partner)

    def activate(q):
        recv(("ps", q))

        for yy in range(SIDE):
            pre = pa[q, yy] + pr[q, yy]
            gate, up = pre[:, 0:hid], pre[:, hid : 2 * hid]
            hidden = gate / (1.0 + jnp.exp(-gate)) * up
            for xx in range(SIDE):
                i = yy * SIDE + xx
                column = gates_t[pl.ds(q * chunk, chunk), pl.ds(i, 1)]
                piece = hidden[xx * chunk : (xx + 1) * chunk] * column
                h_own[q, yy, pl.ds(xx * chunk, chunk), :] = piece.astype(bf16)
        send(("h", q), h_own.at[q], h_oth.at[q], partner)

    def expand(q):
        recv(("h", q))

        def body(i, carry):
            yy = lax.rem(py + 2 + i, SIDE)
            hidden = jnp.concatenate([h_own[q, yy], h_oth[q, yy]], axis=1)
            for h in range(2):
                val = jnp.dot(hidden, w2[:, h * part : (h + 1) * part], preferred_element_type=f32)
                ob[q, h, yy] = val.astype(bf16).reshape(SIDE, chunk, part)
            return carry

        lax.fori_loop(0, SIDE, body, 0)

    index_of = {0: 0, 1: 1, -1: 2, 2: 3}

    def add_half(q, h, da, db, rows_, src):
        yy, xx = place(h, da, db)
        ob[q, h, yy, xx, rows_] = ob[q, h, yy, xx, rows_] + src

    def rs_far(q, a):
        for h in range(2):
            for d in (1, -1):
                src = block(ob, q, h, a, 2, low if d == 1 else high)
                send(("r1", q, h, a, d), src, rh.at[q, h, index_of[a], (1 - d) // 2], xy_device(h, 0, d))

    def rs_side(q, a):
        for h in range(2):
            for d in (1, -1):
                recv(("r1", q, h, a, d))
                add_half(q, h, a, d, low if d == 1 else high, rh[q, h, index_of[a], (1 - d) // 2])
                send(
                    ("r2", q, h, a, d),
                    block(ob, q, h, a, d),
                    rf.at[q, h, index_of[a], (1 - d) // 2],
                    xy_device(h, 0, d),
                )

    def rs_take(q, h, a):
        for d in (1, -1):
            recv(("r2", q, h, a, d))
        i = index_of[a]
        yy, xx = place(h, a, 0)
        total = ob[q, h, yy, xx].astype(f32) + rf[q, h, i, 0].astype(f32) + rf[q, h, i, 1].astype(f32)
        ob[q, h, yy, xx] = total.astype(bf16)

    def rs_second_far(q):
        for h in range(2):
            rs_take(q, h, 2)
            for d in (1, -1):
                src = block(ob, q, h, 2, 0, low if d == 1 else high)
                send(("r3", q, h, d), src, rh.at[q, h, 4, (1 - d) // 2], xy_device(h, d, 0))

    def rs_second_side(q):
        for h in range(2):
            for d in (1, -1):
                rs_take(q, h, d)
                recv(("r3", q, h, d))
                add_half(q, h, d, 0, low if d == 1 else high, rh[q, h, 4, (1 - d) // 2])
                send(("r4", q, h, d), block(ob, q, h, d, 0), rf.at[q, h, 4, (1 - d) // 2], xy_device(h, d, 0))

    def rs_last(q):
        per = part // 128
        for h in range(2):
            rs_take(q, h, 0)
            for d in (1, -1):
                recv(("r4", q, h, d))
            total = ob[q, h, py, px].astype(f32) + rf[q, h, 4, 0].astype(f32) + rf[q, h, 4, 1].astype(f32)
            for i in range(per):
                spread[:, h * per + i, :] = total[:, i * 128 : (i + 1) * 128]
        y3[q] = spread[...].astype(bf16)

    def z_near(q):
        for o in near_offsets:
            src = y3.at[q, pl.ds(lax.rem(r + (o + near), near) * 4, 4)]
            send(("zn", q, o), src, rn.at[q, near_offsets.index(o)], device(ringz(o), core, py, px))

    def z_take(q):
        for o in near_offsets:
            recv(("zn", q, o))
        total = y3[q, pl.ds(r * 4, 4)].astype(f32)
        for i in range(len(near_offsets)):
            total = total + rn[q, i].astype(f32)
        ya[pl.ds(q * 4, 4)] = total.astype(bf16)

    ag_finish(0)
    project(0)
    ag_second_forward(1, 1)
    ag_second_forward(1, -1)
    activate(0)
    ag_second_forward(1, 2)
    expand(0)
    for a in (2, 1, -1, 0):
        rs_far(0, a)
    ag_finish(1)
    project(1)
    rs_side(0, 2)
    activate(1)
    rs_side(0, 1)
    rs_side(0, -1)
    rs_side(0, 0)
    expand(1)
    for a in (2, 1, -1, 0):
        rs_far(1, a)
    rs_second_far(0)
    rs_second_side(0)
    for a in (2, 1, -1, 0):
        rs_side(1, a)
    rs_last(0)
    z_near(0)
    rs_second_far(1)
    rs_second_side(1)
    z_take(0)
    rs_last(1)
    z_near(1)
    z_take(1)

    for dj, dc in far_steps:
        jj, cc, target = far_device(dj, dc)
        send(("zf", dj, dc), ya.at[jj * 2 + cc], rz.at[dj * 2 + dc], target)
    for dj, dc in far_steps:
        recv(("zf", dj, dc))
    same = ya[j * 2 + core].astype(f32)
    cross = jnp.zeros_like(same)
    for dj in range(FAR):
        if dj:
            same = same + rz[dj * 2].astype(f32)
        cross = cross + rz[dj * 2 + 1].astype(f32)
    out[core] = same.astype(bf16)
    out[other] = cross.astype(bf16)

    for copy in sent.values():
        copy.wait_send()


def solution(mesh):
    n_dp = mesh.shape["dp"]

    def shards(tokens, routes, gate_num, w_gate, w_up, w_down):
        feats = tokens.shape[2]
        per_token = routes.shape[2]
        hid = w_down.shape[1]
        experts = mesh.shape["node"] * mesh.shape["innode"]
        ring = 2 * n_dp
        chunk, near = ring, ring // FAR
        tiles, part = feats // 256, feats // 4
        dims = (n_dp, feats, experts, per_token, n_dp * experts)
        tok = tokens.reshape(2, tiles, 128)
        meta = jnp.concatenate([routes[0], gate_num[0]], axis=1).astype(jnp.float32)
        meta = jnp.pad(meta, ((0, 0), (0, 128 - 2 * per_token)))
        bf16, f32 = jnp.bfloat16, jnp.float32
        copies = 400
        vm = pltpu.VMEM
        out, stats = pl.pallas_call(
            functools.partial(kernel, dims),
            out_shape=(
                jax.ShapeDtypeStruct((2, tiles, 128), bf16),
                jax.ShapeDtypeStruct((8, 128), f32),
            ),
            in_specs=[pl.BlockSpec(memory_space=pltpu.VMEM)] * 2 + [pl.BlockSpec(memory_space=pl.ANY)] * 3,
            out_specs=[pl.BlockSpec(memory_space=pltpu.VMEM)] * 2,
            scratch_shapes=[
                vm((2 * chunk, tiles, 128), bf16),
                vm((2, chunk, 1, 128), f32),
                vm((SIDE, SIDE, 2 * per_token, 128), f32),
                vm((chunk, tiles, 128), f32),
                vm((128, 128), f32),
                vm((2, 2, SIDE, SIDE, chunk, part), bf16),
                vm((2, part, 4 * hid), bf16),
                vm((2 * hid, 2 * part), bf16),
                vm((2, SIDE, SIDE * chunk, 2 * hid), f32),
                vm((2, SIDE, SIDE * chunk, 2 * hid), f32),
                vm((2, SIDE, SIDE * chunk, 2 * hid), f32),
                vm((2, SIDE, SIDE * chunk, hid), bf16),
                vm((2, SIDE, SIDE * chunk, hid), bf16),
                vm((128, 128), f32),
                vm((2, 2, SIDE, SIDE, chunk, part), bf16),
                vm((2, 2, 5, 2, chunk // 2, part), bf16),
                vm((2, 2, 5, 2, chunk, part), bf16),
                vm((2, chunk, tiles, 128), bf16),
                vm((2, max(1, near - 1), 4, tiles, 128), bf16),
                vm((8, tiles, 128), bf16),
                vm((8, tiles, 128), bf16),
                pltpu.SemaphoreType.DMA((copies,)),
                pltpu.SemaphoreType.DMA((copies,)),
                pltpu.SemaphoreType.DMA((8,)),
            ],
            compiler_params=pltpu.CompilerParams(
                collective_id=0, has_side_effects=True, vmem_limit_bytes=50 * 1024 * 1024
            ),
            name="expert_layer",
        )(tok, meta, w_gate, w_up, w_down)
        return out.reshape(1, 1, feats), stats[0, :experts], stats[1, 0]

    column = P(("node", "innode"), "dp", None)
    in_specs = (column, column, column, P(("node", "innode"), None, "dp"), P(("node", "innode"), None, "dp"), column)
    return jax.shard_map(shards, mesh=mesh, in_specs=in_specs, out_specs=(column, P(), P()), check_vma=False)
```

```python
import functools

import jax
import jax.numpy as jnp
from jax import lax
from jax.experimental import pallas as pl
from jax.experimental.pallas import tpu as pltpu
from jax.sharding import PartitionSpec as P

GATE_DEN = 256
MESH = pl.DeviceIdType.MESH
SIDE = 4
N_SEND, N_RECV = 33, 102
FAR = 4


def kernel(
    dims,
    tokens,
    routes,
    gate_num,
    wg,
    wu,
    wd,
    out,
    load_out,
    loss_out,
    tok_in,
    routes_in,
    gates_in,
    tok,
    rows_f,
    pair,
    pair_m,
    x3,
    mz,
    codes,
    spread,
    meta_t,
    xb,
    w1,
    w2,
    pa,
    ps,
    pr,
    h_own,
    h_oth,
    gates_t,
    ob,
    rh,
    rf,
    y3,
    rn,
    ya,
    rz,
    fin,
    ssem,
    rsem,
    lsem,
):
    n_dp, feats, experts, per_token, total_tokens = dims
    ring = 2 * n_dp
    near = ring // FAR
    chunk = ring
    half = chunk // 2
    tiles = feats // 256
    part = feats // 4
    hid = wd.shape[1]
    f32, bf16 = jnp.float32, jnp.bfloat16

    dp = lax.axis_index("dp")
    node = lax.axis_index("node")
    inn = lax.axis_index("innode")
    z = lax.div(node, 2) * n_dp + dp
    core = lax.rem(node, 2)
    other = 1 - core
    py = lax.div(inn, SIDE)
    px = lax.rem(inn, SIDE)

    def device(zz, cc, yy, xx):
        return (lax.rem(zz, n_dp), lax.div(zz, n_dp) * 2 + cc, yy * SIDE + xx)

    def ringz(o):
        return lax.rem(z + (o + ring), ring)

    def side(p, o):
        return lax.rem(p + (o + SIDE), SIDE)

    far = [3 * near // 2, -3 * near // 2, near // 2, -near // 2]
    steps = sorted(range(-near // 2, near // 2), key=abs)
    members = 2 * FAR
    per_chunk = near // 2

    def along(o):
        return device(ringz(o), core, py, px)

    partner = device(z, other, py, px)

    barrier = pltpu.get_barrier_semaphore()
    greet = [along(f) for f in far]
    greet += [along(o) for o in range(near // 2, 0, -1)] + [along(-o) for o in range(near // 2, 0, -1)]
    greet = greet if near > 2 else greet[:2] + [along(1), along(-1)]
    greet += [device(z, core, py, side(px, o)) for o in (1, -1)]
    greet += [device(z, core, side(py, o), px) for o in (1, -1)]
    greet += [partner]
    for target in greet:
        pl.semaphore_signal(barrier, inc=1, device_id=target, device_id_type=MESH)

    def load(src, dst, i):
        copy = pltpu.make_async_copy(src, dst, lsem.at[i])
        copy.start()
        return copy

    def rows_of(c, h):
        return pl.ds(pl.multiple_of(c * (2 * part) + h * part, part), part)

    def lanes_of(c):
        return pl.ds(pl.multiple_of(c * (2 * part), 2 * part), 2 * part)

    small = [load(tokens, tok_in, 0), load(routes, routes_in, 1), load(gate_num, gates_in, 2)]
    for h in range(2):
        load(wg.at[0, rows_of(core, h), :], w1.at[h, :, pl.ds(0, hid)], 3)
        load(wu.at[0, rows_of(core, h), :], w1.at[h, :, pl.ds(hid, hid)], 3)
    load(wd.at[0, :, lanes_of(core)], w2.at[pl.ds(0, hid), :], 4)

    for copy in small:
        copy.wait()
    for i in range(2 * tiles):
        rows_f[pl.ds(i, 1), :] = tok_in[0, :, pl.ds(i * 128, 128)].astype(f32)
    for h in range(2):
        tok[h] = rows_f[pl.ds(h * tiles, tiles), :].astype(bf16)
    pair[core] = tok[core]
    pair_m[core] = jnp.concatenate(
        [
            routes_in[0].astype(f32),
            gates_in[0].astype(f32),
            jnp.zeros((1, 128 - 2 * per_token), f32),
        ],
        axis=1,
    )

    pl.semaphore_wait(barrier, len(greet))

    sends, recvs = {}, {}

    def send(name, src, dst, target, arrival=None, departure=None):
        arrival = name if arrival is None else arrival
        departure = name if departure is None else departure
        pltpu.make_async_remote_copy(
            src_ref=src,
            dst_ref=dst,
            send_sem=ssem.at[sends.setdefault(departure, len(sends))],
            recv_sem=rsem.at[recvs.setdefault(arrival, len(recvs))],
            device_id=target,
            device_id_type=MESH,
        ).start()

    def end_of(like, s_index, r_index):
        return pltpu.make_async_remote_copy(
            src_ref=like,
            dst_ref=like,
            send_sem=ssem.at[s_index],
            recv_sem=rsem.at[r_index],
            device_id=partner,
            device_id_type=MESH,
        )

    def arrived(name, like):
        end_of(like, 0, recvs[name]).wait_recv()

    def departed(name, like):
        end_of(like, sends.pop(name), 0).wait_send()

    send("pair", tok.at[other], pair.at[core], partner)
    send("pairm", pair_m.at[core], pair_m.at[core], partner)
    arrived("pair", tok.at[0])
    for i, f in enumerate(far):
        send("far", pair, x3.at[pl.ds(2 * i, 2)], along(f))
    arrived("pairm", pair_m.at[0])
    for i, f in enumerate(far):
        send("farm", pair_m, mz.at[pl.ds(2 * i, 2)], along(f))

    for h in range(2):
        send("w1", wg.at[0, rows_of(other, h), :], w1.at[h, :, pl.ds(2 * hid, hid)], partner)
        send("w1", wu.at[0, rows_of(other, h), :], w1.at[h, :, pl.ds(3 * hid, hid)], partner)
    send("w2", wd.at[0, :, lanes_of(other)], w2.at[pl.ds(hid, hid), :], partner)

    near_rest = pl.ds(members, (near - 1) * members)
    arrived("far", x3.at[pl.ds(0, members)])
    for g in range(1, near):
        send("near", x3.at[pl.ds(0, members)], x3.at[pl.ds(g * members, members)], along(steps[g]), ("near", g // per_chunk))
    arrived("farm", mz.at[pl.ds(0, members)])
    for g in range(1, near):
        send("nearm", mz.at[pl.ds(0, members)], mz.at[pl.ds(g * members, members)], along(steps[g]))

    def place(h, da, db):
        return (side(py, db), side(px, da)) if h == 0 else (side(py, da), side(px, db))

    def xy_device(h, da, db):
        yy, xx = place(h, da, db)
        return device(z, core, yy, xx)

    def block(ref, q, h, da, db, rows=None):
        yy, xx = place(h, da, db)
        return ref.at[q, h, yy, xx] if rows is None else ref.at[q, h, yy, xx, rows]

    low, high = pl.ds(0, half), pl.ds(half, half)

    def ag_own(q):
        for h in range(2):
            for d in (1, -1):
                src = block(xb, q, h, 0, 0)
                send(("p1", q, h), src, src, xy_device(h, d, 0), None, ("full", q, h))
        for h in range(2):
            ag_second(q, h, 0)

    def ag_second(q, h, a):
        src = block(xb, q, h, a, 0)
        for d in (1, -1):
            send(("p2", q, h, a), src, src, xy_device(h, 0, d), None, ("full", q, h))

    def ag_first_forward(q):
        for h in range(2):
            arrived(("p1", q, h), rf.at[q, h, 0])
            for d in (1, -1):
                src = block(xb, q, h, -d, 0, low if d == 1 else high)
                send(("p1f", q, h), src, src, xy_device(h, d, 0), None, ("half", q, h))
            for d in (1, -1):
                ag_second(q, h, -d)

    def ag_second_forward(q, a):
        for h in range(2):
            arrived(("p2", q, h, a), rf.at[q, h, 0])
            for d in (1, -1):
                src = block(xb, q, h, a, -d, low if d == 1 else high)
                send(("p2f", q, h), src, src, xy_device(h, 0, d), None, ("half", q, h))

    def ag_opposite(q):
        for h in range(2):
            arrived(("p1f", q, h), block(xb, q, h, 2, 0))
            ag_second(q, h, 2)

    def ag_finish(q):
        for h in range(2):
            arrived(("p2f", q, h), rh.at[q, h, pl.ds(0, SIDE)])

    def spread_in(q):
        first = members if q == 0 else 0
        arrived(("near", q), x3.at[pl.ds(q * chunk + first, chunk - first)])
        spread[...] = x3[pl.ds(q * chunk, chunk)].astype(f32)
        per = part // 128
        for h in range(2):
            for i in range(per):
                xb[q, h, py, px, :, pl.ds(i * 128, 128)] = spread[:, h * per + i, :].astype(bf16)

    turn = (2, 1, -1, 0)

    def project(q):
        for t in turn:
            yy = side(py, t)
            acc = jnp.dot(xb[q, 0, yy].reshape(SIDE * chunk, part), w1[0], preferred_element_type=f32)
            acc = acc + jnp.dot(xb[q, 1, yy].reshape(SIDE * chunk, part), w1[1], preferred_element_type=f32)
            pa[q, yy] = acc[:, 0 : 2 * hid]
            ps[q, yy] = acc[:, 2 * hid : 4 * hid]
            send(("ps", q, t), ps.at[q, yy], pr.at[q, yy], partner, None, ("ps", q))

    def activate(q):
        for t in turn:
            yy = side(py, t)
            arrived(("ps", q, t), ps.at[q, 0])
            pre = pa[q, yy] + pr[q, yy]
            gate, up = pre[:, 0:hid], pre[:, hid : 2 * hid]
            hidden = gate / (1.0 + jnp.exp(-gate)) * up
            for xx in range(SIDE):
                column = gates_t[q, yy, pl.ds(xx * chunk, chunk), :]
                piece = hidden[xx * chunk : (xx + 1) * chunk] * column
                h_own[q, yy, pl.ds(xx * chunk, chunk), :] = piece.astype(bf16)
            send(("h", q, t), h_own.at[q, yy], h_oth.at[q, yy], partner, None, ("h", q))

    index_of = {0: 0, 1: 1, -1: 2, 2: 3}

    def expand(q):
        for t in turn:
            yy = side(py, t)
            arrived(("h", q, t), h_own.at[q, 0])
            hidden = jnp.concatenate([h_own[q, yy], h_oth[q, yy]], axis=1)
            for h in range(2):
                val = jnp.dot(hidden, w2[:, h * part : (h + 1) * part], preferred_element_type=f32)
                ob[q, h, yy] = val.astype(bf16).reshape(SIDE, chunk, part)
            if t == 2:
                for a in turn:
                    rs_far(q, 0, a)
            rs_far(q, 1, t)

    def rs_far(q, h, a):
        for d in (1, -1):
            src = block(ob, q, h, a, 2, low if d == 1 else high)
            dst = rh.at[q, h, index_of[a], (1 - d) // 2]
            send(("r1", q, h, a), src, dst, xy_device(h, 0, d), None, ("rhalf", q, h))

    def add_half(q, h, da, db, rows, src):
        yy, xx = place(h, da, db)
        ob[q, h, yy, xx, rows] = ob[q, h, yy, xx, rows] + src

    def rs_side(q, a):
        for h in range(2):
            i = index_of[a]
            arrived(("r1", q, h, a), rh.at[q, h, i])
            for d in (1, -1):
                add_half(q, h, a, d, low if d == 1 else high, rh[q, h, i, (1 - d) // 2])
                dst = rf.at[q, h, i, (1 - d) // 2]
                send(("r2", q, h, a), block(ob, q, h, a, d), dst, xy_device(h, 0, d), None, ("rfull", q, h))

    def rs_take(q, h, a):
        i = index_of[a]
        arrived(("r2", q, h, a), rf.at[q, h, i])
        yy, xx = place(h, a, 0)
        return ob[q, h, yy, xx].astype(f32) + rf[q, h, i, 0].astype(f32) + rf[q, h, i, 1].astype(f32)

    def rs_second_far(q):
        for h in range(2):
            yy, xx = place(h, 2, 0)
            ob[q, h, yy, xx] = rs_take(q, h, 2).astype(bf16)
            for d in (1, -1):
                src = block(ob, q, h, 2, 0, low if d == 1 else high)
                dst = rh.at[q, h, 4, (1 - d) // 2]
                send(("r3", q, h), src, dst, xy_device(h, d, 0), None, ("rhalf", q, h))

    def rs_second_side(q):
        for h in range(2):
            for d in (1, -1):
                yy, xx = place(h, d, 0)
                ob[q, h, yy, xx] = rs_take(q, h, d).astype(bf16)
        for h in range(2):
            arrived(("r3", q, h), rh.at[q, h, 4])
            for d in (1, -1):
                add_half(q, h, d, 0, low if d == 1 else high, rh[q, h, 4, (1 - d) // 2])
                dst = rf.at[q, h, 4, (1 - d) // 2]
                send(("r4", q, h), block(ob, q, h, d, 0), dst, xy_device(h, d, 0), None, ("rfull", q, h))

    def rs_last(q):
        per = part // 128
        for h in range(2):
            total = rs_take(q, h, 0)
            arrived(("r4", q, h), rf.at[q, h, 4])
            total = total + rf[q, h, 4, 0].astype(f32) + rf[q, h, 4, 1].astype(f32)
            for i in range(per):
                spread[:, h * per + i, :] = total[:, i * 128 : (i + 1) * 128]
        y3[q] = spread[...].astype(bf16)
        for g in range(q * per_chunk, (q + 1) * per_chunk):
            if g:
                src = y3.at[q, pl.ds((g - q * per_chunk) * members, members)]
                send("zn", src, rn.at[g - 1], along(-steps[g]))

    def statistics():
        rows_e = lax.broadcasted_iota(jnp.int32, (experts, 128), 0).astype(f32)

        def body(i, carry):
            counts, share_sums = carry
            table = codes[lax.div(i, SIDE), lax.rem(i, SIDE)]
            route, numer = table[0:per_token], table[per_token : 2 * per_token]
            numer = jnp.where(route >= 0, numer, 0.0)
            total = jnp.sum(numer, axis=0, keepdims=True)
            share = numer / jnp.where(total > 0, total, 1.0)
            for k in range(per_token):
                hit = rows_e == route[k : k + 1]
                counts = counts + jnp.where(hit, 1.0, 0.0)
                share_sums = share_sums + jnp.where(hit, share[k : k + 1], 0.0)
            return counts, share_sums

        zero = jnp.zeros((experts, 128), f32)
        counts, share_sums = lax.fori_loop(0, SIDE * SIDE, body, (zero, zero))
        load_col = jnp.sum(counts, axis=1, keepdims=True) * (experts / (per_token * total_tokens))
        mean_col = jnp.sum(share_sums, axis=1, keepdims=True) / total_tokens
        meta_t[pl.ds(0, experts), :] = jnp.broadcast_to(load_col, (experts, 128))
        load_out[...] = jnp.transpose(meta_t[...])[0:1, 0:experts]
        loss_out[...] = jnp.sum(load_col * mean_col, axis=0, keepdims=True)

    def codes_own():
        arrived("nearm", mz.at[near_rest])
        meta_t[...] = jnp.full_like(meta_t, -1.0)
        meta_t[pl.ds(0, 2 * chunk), :] = mz[:, 0, :]
        codes[py, px] = jnp.transpose(meta_t[...])[0 : 2 * per_token]
        for o in (1, -1):
            src = codes.at[py, px]
            send(("mx", o), src, src, device(z, core, py, side(px, o)), None, "mx")

    def codes_x():
        arrived(("mx", 1), codes.at[0, 0])
        src = codes.at[py, side(px, -1)]
        send(("mx", 2), src, src, device(z, core, py, side(px, 1)), None, "mx")

    def codes_row():
        arrived(("mx", -1), codes.at[0, 0])
        arrived(("mx", 2), codes.at[0, 0])
        for o in (1, -1):
            src = codes.at[py]
            send(("my", o), src, src, device(z, core, side(py, o), px), None, "my")

    def codes_y():
        arrived(("my", 1), codes.at[0])
        src = codes.at[side(py, -1)]
        send(("my", 2), src, src, device(z, core, side(py, 1), px), None, "my")

    def gates():
        arrived(("my", -1), codes.at[0])
        arrived(("my", 2), codes.at[0])
        expert = (node * (SIDE * SIDE) + inn).astype(f32)
        meta_t[...] = jnp.zeros_like(meta_t)
        for yy in range(SIDE):
            for xx in range(SIDE):
                route, numer = codes[yy, xx, 0:per_token], codes[yy, xx, per_token : 2 * per_token]
                meta_t[pl.ds(yy * SIDE + xx, 1), :] = jnp.sum(
                    jnp.where(route == expert, numer, 0.0), axis=0, keepdims=True
                ) * (1.0 / GATE_DEN)
        columns = jnp.transpose(meta_t[...])
        for q in range(2):
            for yy in range(SIDE):
                for xx in range(SIDE):
                    i = yy * SIDE + xx
                    column = columns[q * chunk : (q + 1) * chunk, i : i + 1]
                    gates_t[q, yy, pl.ds(xx * chunk, chunk), :] = jnp.broadcast_to(column, (chunk, hid))

    spread_in(0)
    ag_own(0)
    spread_in(1)
    ag_own(1)
    codes_own()
    ag_first_forward(0)
    ag_second_forward(0, 0)
    ag_opposite(0)
    codes_x()
    ag_first_forward(1)
    ag_second_forward(0, 1)
    ag_second_forward(0, -1)
    codes_row()
    ag_second_forward(1, 0)
    ag_opposite(1)
    ag_second_forward(0, 2)
    codes_y()
    pltpu.make_async_copy(w1.at[:, :, pl.ds(0, 2 * hid)], w1.at[:, :, pl.ds(0, 2 * hid)], lsem.at[3]).wait()
    pltpu.make_async_copy(w2.at[pl.ds(0, hid), :], w2.at[pl.ds(0, hid), :], lsem.at[4]).wait()
    arrived("w1", w1.at[:, :, pl.ds(2 * hid, 2 * hid)])
    arrived("w2", w2.at[pl.ds(hid, hid), :])
    gates()

    ag_finish(0)
    project(0)
    ag_second_forward(1, 1)
    ag_second_forward(1, -1)
    activate(0)
    ag_second_forward(1, 2)
    expand(0)
    ag_finish(1)
    project(1)
    rs_side(0, 2)
    activate(1)
    rs_side(0, 1)
    rs_side(0, -1)
    rs_side(0, 0)
    expand(1)
    rs_second_far(0)
    rs_second_side(0)
    rs_side(1, 2)
    rs_side(1, 1)
    rs_side(1, -1)
    rs_side(1, 0)
    rs_last(0)
    rs_second_far(1)
    rs_second_side(1)
    rs_last(1)

    arrived("zn", rn)
    total = y3[0, pl.ds(0, members)].astype(f32)
    for g in range(near - 1):
        total = total + rn[g].astype(f32)
    ya[...] = total.astype(bf16)
    for i, f in enumerate(far):
        send("zf", ya.at[pl.ds(2 * i, 2)], rz.at[i], along(-f))
    statistics()
    for q in range(2):
        for h in range(2):
            departed(("full", q, h), rf.at[q, h])
            departed(("half", q, h), rh.at[q, h])
            departed(("rfull", q, h), rf.at[q, h])
            departed(("rhalf", q, h), rh.at[q, h])
        departed(("ps", q), ps.at[q])
        departed(("h", q), h_own.at[q])
    departed("pair", tok.at[0])
    departed("pairm", pair_m.at[0])
    departed("far", x3.at[pl.ds(0, members)])
    departed("farm", mz.at[pl.ds(0, members)])
    departed("near", x3.at[near_rest])
    departed("nearm", mz.at[near_rest])
    departed("w1", w1.at[:, :, pl.ds(2 * hid, 2 * hid)])
    departed("w2", w2.at[pl.ds(hid, hid), :])
    departed("mx", codes.at[0, pl.ds(0, 3)])
    departed("my", codes.at[pl.ds(0, 3)])
    departed("zn", rn)
    departed("zf", rz)
    arrived("zf", rz)

    def gathered(c):
        return rz[0, c].astype(f32) + rz[1, c].astype(f32) + rz[2, c].astype(f32) + rz[3, c].astype(f32)

    fin[other] = gathered(other).astype(bf16)
    send("fin", fin.at[other], fin.at[other], partner)
    rows_f[pl.ds(pl.multiple_of(core * tiles, tiles), tiles), :] = gathered(core)
    arrived("fin", fin.at[0])
    rows_f[pl.ds(pl.multiple_of(other * tiles, tiles), tiles), :] = fin[core].astype(f32)
    for i in range(2 * tiles):
        out[0, :, pl.ds(i * 128, 128)] = rows_f[pl.ds(i, 1), :].astype(bf16)
    departed("fin", fin.at[0])


def solution(mesh):
    n_dp = mesh.shape["dp"]

    def shards(tokens, routes, gate_num, w_gate, w_up, w_down):
        feats = tokens.shape[2]
        per_token = routes.shape[2]
        hid = w_down.shape[1]
        experts = mesh.shape["node"] * mesh.shape["innode"]
        ring = 2 * n_dp
        chunk, near = ring, ring // FAR
        tiles, part = feats // 256, feats // 4
        dims = (n_dp, feats, experts, per_token, n_dp * experts)
        bf16, f32 = jnp.bfloat16, jnp.float32
        vm = pltpu.VMEM
        out, load, loss = pl.pallas_call(
            functools.partial(kernel, dims),
            out_shape=(
                jax.ShapeDtypeStruct((1, 1, feats), bf16),
                jax.ShapeDtypeStruct((1, experts), f32),
                jax.ShapeDtypeStruct((1, 1), f32),
            ),
            in_specs=[pl.BlockSpec(memory_space=pltpu.HBM)] * 6,
            out_specs=[pl.BlockSpec(memory_space=pltpu.VMEM)] * 3,
            scratch_shapes=[
                vm((1, 1, feats), bf16),
                vm((1, 1, per_token), jnp.int32),
                vm((1, 1, per_token), jnp.int32),
                vm((2, tiles, 128), bf16),
                vm((2 * tiles, 128), f32),
                vm((2, tiles, 128), bf16),
                vm((2, 1, 128), f32),
                vm((2 * chunk, tiles, 128), bf16),
                vm((2 * chunk, 1, 128), f32),
                vm((SIDE, SIDE, 2 * per_token, 128), f32),
                vm((chunk, tiles, 128), f32),
                vm((128, 128), f32),
                vm((2, 2, SIDE, SIDE, chunk, part), bf16),
                vm((2, part, 4 * hid), bf16),
                vm((2 * hid, 2 * part), bf16),
                vm((2, SIDE, SIDE * chunk, 2 * hid), f32),
                vm((2, SIDE, SIDE * chunk, 2 * hid), f32),
                vm((2, SIDE, SIDE * chunk, 2 * hid), f32),
                vm((2, SIDE, SIDE * chunk, hid), bf16),
                vm((2, SIDE, SIDE * chunk, hid), bf16),
                vm((2, SIDE, SIDE * chunk, hid), f32),
                vm((2, 2, SIDE, SIDE, chunk, part), bf16),
                vm((2, 2, 5, 2, chunk // 2, part), bf16),
                vm((2, 2, 5, 2, chunk, part), bf16),
                vm((2, chunk, tiles, 128), bf16),
                vm((near - 1, 2 * FAR, tiles, 128), bf16),
                vm((2 * FAR, tiles, 128), bf16),
                vm((FAR, 2, tiles, 128), bf16),
                vm((2, tiles, 128), bf16),
                pltpu.SemaphoreType.DMA((N_SEND,)),
                pltpu.SemaphoreType.DMA((N_RECV,)),
                pltpu.SemaphoreType.DMA((5,)),
            ],
            compiler_params=pltpu.CompilerParams(
                collective_id=0, has_side_effects=True, vmem_limit_bytes=63 * 1024 * 1024
            ),
            name="expert_layer",
        )(tokens, routes, gate_num, w_gate, w_up, w_down)
        return out, load.reshape(experts), loss.reshape(())

    column = P(("node", "innode"), "dp", None)
    in_specs = (column, column, column, P(("node", "innode"), None, "dp"), P(("node", "innode"), None, "dp"), column)
    return jax.shard_map(shards, mesh=mesh, in_specs=in_specs, out_specs=(column, P(), P()), check_vma=False)
```

```python
import functools

import jax
import jax.numpy as jnp
from jax import lax
from jax.experimental import pallas as pl
from jax.experimental.pallas import tpu as pltpu
from jax.sharding import PartitionSpec as P

GATE_DEN = 256
MESH = pl.DeviceIdType.MESH
SIDE = 4
N_SEND, N_RECV = 33, 98
FAR = 4


def kernel(
    dims,
    tokens,
    routes,
    gate_num,
    wg,
    wu,
    wd,
    out,
    load_out,
    loss_out,
    tok_in,
    routes_in,
    gates_in,
    tok,
    rows_f,
    pair,
    pair_m,
    x3,
    mz,
    codes,
    spread,
    meta_t,
    xb,
    w1,
    w2,
    pa,
    ps,
    pr,
    h_own,
    h_oth,
    gates_t,
    ob,
    rh,
    rf,
    y3,
    rn,
    ya,
    rz,
    fin,
    ssem,
    rsem,
    lsem,
):
    n_dp, feats, experts, per_token, total_tokens = dims
    ring = 2 * n_dp
    near = ring // FAR
    chunk = ring
    half = chunk // 2
    tiles = feats // 256
    part = feats // 4
    hid = wd.shape[1]
    f32, bf16 = jnp.float32, jnp.bfloat16

    dp = lax.axis_index("dp")
    node = lax.axis_index("node")
    inn = lax.axis_index("innode")
    z = lax.div(node, 2) * n_dp + dp
    core = lax.rem(node, 2)
    other = 1 - core
    py = lax.div(inn, SIDE)
    px = lax.rem(inn, SIDE)

    def device(zz, cc, yy, xx):
        return (lax.rem(zz, n_dp), lax.div(zz, n_dp) * 2 + cc, yy * SIDE + xx)

    def ringz(o):
        return lax.rem(z + (o + ring), ring)

    def side(p, o):
        return lax.rem(p + (o + SIDE), SIDE)

    far = [3 * near // 2, -3 * near // 2, near // 2, -near // 2]
    steps = sorted(range(-near // 2, near // 2), key=abs)
    members = 2 * FAR
    per_chunk = near // 2

    def along(o):
        return device(ringz(o), core, py, px)

    partner = device(z, other, py, px)

    barrier = pltpu.get_barrier_semaphore()
    greet = [along(f) for f in far]
    greet += [along(o) for o in range(near // 2, 0, -1)] + [along(-o) for o in range(near // 2, 0, -1)]
    greet = greet if near > 2 else greet[:2] + [along(1), along(-1)]
    greet += [device(z, core, py, side(px, o)) for o in (2, 1, -1)]
    greet += [device(z, core, side(py, o), px) for o in (2, 1, -1)]
    greet += [partner]
    for target in greet:
        pl.semaphore_signal(barrier, inc=1, device_id=target, device_id_type=MESH)

    def load(src, dst, i):
        copy = pltpu.make_async_copy(src, dst, lsem.at[i])
        copy.start()
        return copy

    def rows_of(c, h):
        return pl.ds(pl.multiple_of(c * (2 * part) + h * part, part), part)

    def lanes_of(c):
        return pl.ds(pl.multiple_of(c * (2 * part), 2 * part), 2 * part)

    small = [load(tokens, tok_in, 0), load(routes, routes_in, 1), load(gate_num, gates_in, 2)]
    for h in range(2):
        load(wg.at[0, rows_of(core, h), :], w1.at[h, :, pl.ds(0, hid)], 3)
        load(wu.at[0, rows_of(core, h), :], w1.at[h, :, pl.ds(hid, hid)], 3)
    load(wd.at[0, :, lanes_of(core)], w2.at[pl.ds(0, hid), :], 4)

    for copy in small:
        copy.wait()
    for i in range(2 * tiles):
        rows_f[pl.ds(i, 1), :] = tok_in[0, :, pl.ds(i * 128, 128)].astype(f32)
    for h in range(2):
        tok[h] = rows_f[pl.ds(h * tiles, tiles), :].astype(bf16)
    pair[core] = tok[core]
    pair_m[core] = jnp.concatenate(
        [
            routes_in[0].astype(f32),
            gates_in[0].astype(f32),
            jnp.zeros((1, 128 - 2 * per_token), f32),
        ],
        axis=1,
    )

    pl.semaphore_wait(barrier, len(greet))

    sends, recvs = {}, {}

    def send(name, src, dst, target, arrival=None, departure=None):
        arrival = name if arrival is None else arrival
        departure = name if departure is None else departure
        pltpu.make_async_remote_copy(
            src_ref=src,
            dst_ref=dst,
            send_sem=ssem.at[sends.setdefault(departure, len(sends))],
            recv_sem=rsem.at[recvs.setdefault(arrival, len(recvs))],
            device_id=target,
            device_id_type=MESH,
        ).start()

    def end_of(like, s_index, r_index):
        return pltpu.make_async_remote_copy(
            src_ref=like,
            dst_ref=like,
            send_sem=ssem.at[s_index],
            recv_sem=rsem.at[r_index],
            device_id=partner,
            device_id_type=MESH,
        )

    def arrived(name, like):
        end_of(like, 0, recvs[name]).wait_recv()

    def departed(name, like):
        end_of(like, sends.pop(name), 0).wait_send()

    send("pair", tok.at[other], pair.at[core], partner)
    send("pairm", pair_m.at[core], pair_m.at[core], partner)
    arrived("pair", tok.at[0])
    for i, f in enumerate(far):
        send("far", pair, x3.at[pl.ds(2 * i, 2)], along(f))
    arrived("pairm", pair_m.at[0])
    for i, f in enumerate(far):
        send("farm", pair_m, mz.at[pl.ds(2 * i, 2)], along(f))

    for h in range(2):
        send("w1", wg.at[0, rows_of(other, h), :], w1.at[h, :, pl.ds(2 * hid, hid)], partner)
        send("w1", wu.at[0, rows_of(other, h), :], w1.at[h, :, pl.ds(3 * hid, hid)], partner)
    send("w2", wd.at[0, :, lanes_of(other)], w2.at[pl.ds(hid, hid), :], partner)

    near_rest = pl.ds(members, (near - 1) * members)
    arrived("far", x3.at[pl.ds(0, members)])
    for g in range(1, near):
        send("near", x3.at[pl.ds(0, members)], x3.at[pl.ds(g * members, members)], along(steps[g]), ("near", g // per_chunk))
    arrived("farm", mz.at[pl.ds(0, members)])
    for g in range(1, near):
        send("nearm", mz.at[pl.ds(0, members)], mz.at[pl.ds(g * members, members)], along(steps[g]))

    def place(h, da, db):
        return (side(py, db), side(px, da)) if h == 0 else (side(py, da), side(px, db))

    def xy_device(h, da, db):
        yy, xx = place(h, da, db)
        return device(z, core, yy, xx)

    def block(ref, q, h, da, db, rows=None):
        yy, xx = place(h, da, db)
        return ref.at[q, h, yy, xx] if rows is None else ref.at[q, h, yy, xx, rows]

    low, high = pl.ds(0, half), pl.ds(half, half)

    def ag_own(q):
        for h in range(2):
            for d in (1, -1):
                src = block(xb, q, h, 0, 0)
                send(("p1", q, h), src, src, xy_device(h, d, 0), None, ("full", q, h))

    def ag_middle(q):
        for h in range(2):
            ag_second(q, h, 0)

    def ag_second(q, h, a):
        src = block(xb, q, h, a, 0)
        for d in (1, -1):
            send(("p2", q, h, a), src, src, xy_device(h, 0, d), None, ("full", q, h))

    def ag_first_forward(q):
        for h in range(2):
            arrived(("p1", q, h), rf.at[q, h, 0])
            for d in (1, -1):
                src = block(xb, q, h, -d, 0, low if d == 1 else high)
                send(("p1f", q, h), src, src, xy_device(h, d, 0), None, ("half", q, h))

    def ag_sides(q):
        for d in (1, -1):
            for h in range(2):
                ag_second(q, h, d)

    def ag_second_forward(q, a):
        for h in range(2):
            arrived(("p2", q, h, a), rf.at[q, h, 0])
            for d in (1, -1):
                src = block(xb, q, h, a, -d, low if d == 1 else high)
                send(("p2f", q, h), src, src, xy_device(h, 0, d), None, ("half", q, h))

    def ag_opposite(q):
        for h in range(2):
            arrived(("p1f", q, h), block(xb, q, h, 2, 0))
            ag_second(q, h, 2)

    def ag_finish(q):
        for h in range(2):
            arrived(("p2f", q, h), rh.at[q, h, pl.ds(0, SIDE)])

    def spread_in(q):
        first = members if q == 0 else 0
        arrived(("near", q), x3.at[pl.ds(q * chunk + first, chunk - first)])
        spread[...] = x3[pl.ds(q * chunk, chunk)].astype(f32)
        per = part // 128
        for h in range(2):
            for i in range(per):
                xb[q, h, py, px, :, pl.ds(i * 128, 128)] = spread[:, h * per + i, :].astype(bf16)

    turn = (2, 1, -1, 0)

    def project(q):
        rows = SIDE * SIDE * chunk
        acc = jnp.dot(xb[q, 0].reshape(rows, part), w1[0], preferred_element_type=f32)
        acc = acc + jnp.dot(xb[q, 1].reshape(rows, part), w1[1], preferred_element_type=f32)
        ps[q] = acc[:, 2 * hid : 4 * hid].reshape(SIDE, SIDE * chunk, 2 * hid)
        for t in turn:
            yy = side(py, t)
            send(("ps", q, t), ps.at[q, yy], pr.at[q, yy], partner, None, ("ps", q))
        pa[q] = acc[:, 0 : 2 * hid].reshape(SIDE, SIDE * chunk, 2 * hid)

    def activate(q):
        for t in turn:
            yy = side(py, t)
            arrived(("ps", q, t), ps.at[q, 0])
            pre = pa[q, yy] + pr[q, yy]
            gate, up = pre[:, 0:hid], pre[:, hid : 2 * hid]
            hidden = gate / (1.0 + jnp.exp(-gate)) * up
            for xx in range(SIDE):
                column = gates_t[q, yy, pl.ds(xx * chunk, chunk), :]
                piece = hidden[xx * chunk : (xx + 1) * chunk] * column
                h_own[q, yy, pl.ds(xx * chunk, chunk), :] = piece.astype(bf16)
            send(("h", q, t), h_own.at[q, yy], h_oth.at[q, yy], partner, None, ("h", q))

    index_of = {0: 0, 1: 1, -1: 2, 2: 3}

    def expand(q):
        for t in turn:
            yy = side(py, t)
            arrived(("h", q, t), h_own.at[q, 0])
            hidden = jnp.concatenate([h_own[q, yy], h_oth[q, yy]], axis=1)
            for h in range(2):
                val = jnp.dot(hidden, w2[:, h * part : (h + 1) * part], preferred_element_type=f32)
                ob[q, h, yy] = val.astype(bf16).reshape(SIDE, chunk, part)
            if t == 2:
                for a in turn:
                    rs_far(q, 0, a)
            rs_far(q, 1, t)

    def rs_far(q, h, a):
        for d in (1, -1):
            src = block(ob, q, h, a, 2, low if d == 1 else high)
            dst = rh.at[q, h, index_of[a], (1 - d) // 2]
            send(("r1", q, h, a), src, dst, xy_device(h, 0, d), None, ("rhalf", q, h))

    def add_half(q, h, da, db, rows, src):
        yy, xx = place(h, da, db)
        ob[q, h, yy, xx, rows] = ob[q, h, yy, xx, rows] + src

    def rs_side(q, a):
        for h in range(2):
            i = index_of[a]
            arrived(("r1", q, h, a), rh.at[q, h, i])
            for d in (1, -1):
                add_half(q, h, a, d, low if d == 1 else high, rh[q, h, i, (1 - d) // 2])
                dst = rf.at[q, h, i, (1 - d) // 2]
                send(("r2", q, h, a), block(ob, q, h, a, d), dst, xy_device(h, 0, d), None, ("rfull", q, h))

    def rs_take(q, h, a):
        i = index_of[a]
        arrived(("r2", q, h, a), rf.at[q, h, i])
        yy, xx = place(h, a, 0)
        return ob[q, h, yy, xx].astype(f32) + rf[q, h, i, 0].astype(f32) + rf[q, h, i, 1].astype(f32)

    def rs_second_far(q):
        for h in range(2):
            yy, xx = place(h, 2, 0)
            ob[q, h, yy, xx] = rs_take(q, h, 2).astype(bf16)
            for d in (1, -1):
                src = block(ob, q, h, 2, 0, low if d == 1 else high)
                dst = rh.at[q, h, 4, (1 - d) // 2]
                send(("r3", q, h), src, dst, xy_device(h, d, 0), None, ("rhalf", q, h))

    def rs_second_side(q):
        for h in range(2):
            for d in (1, -1):
                yy, xx = place(h, d, 0)
                ob[q, h, yy, xx] = rs_take(q, h, d).astype(bf16)
        for h in range(2):
            arrived(("r3", q, h), rh.at[q, h, 4])
            for d in (1, -1):
                add_half(q, h, d, 0, low if d == 1 else high, rh[q, h, 4, (1 - d) // 2])
                dst = rf.at[q, h, 4, (1 - d) // 2]
                send(("r4", q, h), block(ob, q, h, d, 0), dst, xy_device(h, d, 0), None, ("rfull", q, h))

    def rs_last(q):
        per = part // 128
        for h in range(2):
            total = rs_take(q, h, 0)
            arrived(("r4", q, h), rf.at[q, h, 4])
            total = total + rf[q, h, 4, 0].astype(f32) + rf[q, h, 4, 1].astype(f32)
            for i in range(per):
                spread[:, h * per + i, :] = total[:, i * 128 : (i + 1) * 128]
        y3[q] = spread[...].astype(bf16)
        for g in range(q * per_chunk, (q + 1) * per_chunk):
            if g:
                src = y3.at[q, pl.ds((g - q * per_chunk) * members, members)]
                send("zn", src, rn.at[g - 1], along(-steps[g]))

    def statistics():
        rows_e = lax.broadcasted_iota(jnp.int32, (experts, 128), 0).astype(f32)

        def body(i, carry):
            counts, share_sums = carry
            table = codes[lax.div(i, SIDE), lax.rem(i, SIDE)]
            route, numer = table[0:per_token], table[per_token : 2 * per_token]
            numer = jnp.where(route >= 0, numer, 0.0)
            total = jnp.sum(numer, axis=0, keepdims=True)
            share = numer / jnp.where(total > 0, total, 1.0)
            for k in range(per_token):
                hit = rows_e == route[k : k + 1]
                counts = counts + jnp.where(hit, 1.0, 0.0)
                share_sums = share_sums + jnp.where(hit, share[k : k + 1], 0.0)
            return counts, share_sums

        zero = jnp.zeros((experts, 128), f32)
        counts, share_sums = lax.fori_loop(0, SIDE * SIDE, body, (zero, zero))
        load_col = jnp.sum(counts, axis=1, keepdims=True) * (experts / (per_token * total_tokens))
        mean_col = jnp.sum(share_sums, axis=1, keepdims=True) / total_tokens
        meta_t[pl.ds(0, experts), :] = jnp.broadcast_to(load_col, (experts, 128))
        load_out[...] = jnp.transpose(meta_t[...])[0:1, 0:experts]
        loss_out[...] = jnp.sum(load_col * mean_col, axis=0, keepdims=True)

    def codes_own():
        arrived("nearm", mz.at[near_rest])
        meta_t[...] = jnp.full_like(meta_t, -1.0)
        meta_t[pl.ds(0, 2 * chunk), :] = mz[:, 0, :]
        codes[py, px] = jnp.transpose(meta_t[...])[0 : 2 * per_token]
        for o in (2, 1, -1):
            src = codes.at[py, px]
            send("mx", src, src, device(z, core, py, side(px, o)))

    def codes_row():
        arrived("mx", codes.at[0, pl.ds(0, 3)])
        for o in (2, 1, -1):
            src = codes.at[py]
            send("my", src, src, device(z, core, side(py, o), px))

    def gates():
        arrived("my", codes.at[pl.ds(0, 3)])
        expert = (node * (SIDE * SIDE) + inn).astype(f32)
        meta_t[...] = jnp.zeros_like(meta_t)
        for yy in range(SIDE):
            for xx in range(SIDE):
                route, numer = codes[yy, xx, 0:per_token], codes[yy, xx, per_token : 2 * per_token]
                meta_t[pl.ds(yy * SIDE + xx, 1), :] = jnp.sum(
                    jnp.where(route == expert, numer, 0.0), axis=0, keepdims=True
                ) * (1.0 / GATE_DEN)
        columns = jnp.transpose(meta_t[...])
        for q in range(2):
            for yy in range(SIDE):
                for xx in range(SIDE):
                    i = yy * SIDE + xx
                    column = columns[q * chunk : (q + 1) * chunk, i : i + 1]
                    gates_t[q, yy, pl.ds(xx * chunk, chunk), :] = jnp.broadcast_to(column, (chunk, hid))

    spread_in(0)
    ag_own(0)
    ag_middle(0)
    spread_in(1)
    ag_own(1)
    codes_own()
    ag_first_forward(0)
    ag_sides(0)
    ag_first_forward(1)
    ag_middle(1)
    ag_opposite(0)
    ag_opposite(1)
    ag_second_forward(0, 0)
    ag_second_forward(0, 1)
    ag_second_forward(0, -1)
    ag_sides(1)
    codes_row()
    ag_second_forward(0, 2)
    ag_second_forward(1, 0)
    ag_second_forward(1, 2)
    pltpu.make_async_copy(w1.at[:, :, pl.ds(0, 2 * hid)], w1.at[:, :, pl.ds(0, 2 * hid)], lsem.at[3]).wait()
    pltpu.make_async_copy(w2.at[pl.ds(0, hid), :], w2.at[pl.ds(0, hid), :], lsem.at[4]).wait()
    arrived("w1", w1.at[:, :, pl.ds(2 * hid, 2 * hid)])
    arrived("w2", w2.at[pl.ds(hid, hid), :])
    ag_finish(0)
    project(0)
    ag_second_forward(1, 1)
    ag_second_forward(1, -1)
    gates()
    activate(0)
    expand(0)
    ag_finish(1)
    project(1)
    rs_side(0, 2)
    rs_side(0, 1)
    rs_side(0, -1)
    activate(1)
    rs_side(0, 0)
    rs_second_far(0)
    expand(1)
    rs_second_side(0)
    rs_side(1, 2)
    rs_side(1, 1)
    rs_side(1, -1)
    rs_second_far(1)
    rs_side(1, 0)
    rs_last(0)
    rs_second_side(1)
    rs_last(1)

    arrived("zn", rn)
    total = y3[0, pl.ds(0, members)].astype(f32)
    for g in range(near - 1):
        total = total + rn[g].astype(f32)
    ya[...] = total.astype(bf16)
    for i, f in enumerate(far):
        send("zf", ya.at[pl.ds(2 * i, 2)], rz.at[i], along(-f))
    statistics()
    for q in range(2):
        for h in range(2):
            departed(("full", q, h), rf.at[q, h])
            departed(("half", q, h), rh.at[q, h])
            departed(("rfull", q, h), rf.at[q, h])
            departed(("rhalf", q, h), rh.at[q, h])
        departed(("ps", q), ps.at[q])
        departed(("h", q), h_own.at[q])
    departed("pair", tok.at[0])
    departed("pairm", pair_m.at[0])
    departed("far", x3.at[pl.ds(0, members)])
    departed("farm", mz.at[pl.ds(0, members)])
    departed("near", x3.at[near_rest])
    departed("nearm", mz.at[near_rest])
    departed("w1", w1.at[:, :, pl.ds(2 * hid, 2 * hid)])
    departed("w2", w2.at[pl.ds(hid, hid), :])
    departed("mx", codes.at[0, pl.ds(0, 3)])
    departed("my", codes.at[pl.ds(0, 3)])
    departed("zn", rn)
    departed("zf", rz)
    arrived("zf", rz)

    def gathered(c):
        return rz[0, c].astype(f32) + rz[1, c].astype(f32) + rz[2, c].astype(f32) + rz[3, c].astype(f32)

    fin[other] = gathered(other).astype(bf16)
    send("fin", fin.at[other], fin.at[other], partner)
    rows_f[pl.ds(pl.multiple_of(core * tiles, tiles), tiles), :] = gathered(core)
    arrived("fin", fin.at[0])
    rows_f[pl.ds(pl.multiple_of(other * tiles, tiles), tiles), :] = fin[core].astype(f32)
    for i in range(2 * tiles):
        out[0, :, pl.ds(i * 128, 128)] = rows_f[pl.ds(i, 1), :].astype(bf16)
    departed("fin", fin.at[0])


def solution(mesh):
    n_dp = mesh.shape["dp"]

    def shards(tokens, routes, gate_num, w_gate, w_up, w_down):
        feats = tokens.shape[2]
        per_token = routes.shape[2]
        hid = w_down.shape[1]
        experts = mesh.shape["node"] * mesh.shape["innode"]
        ring = 2 * n_dp
        chunk, near = ring, ring // FAR
        tiles, part = feats // 256, feats // 4
        dims = (n_dp, feats, experts, per_token, n_dp * experts)
        bf16, f32 = jnp.bfloat16, jnp.float32
        vm = pltpu.VMEM
        out, load, loss = pl.pallas_call(
            functools.partial(kernel, dims),
            out_shape=(
                jax.ShapeDtypeStruct((1, 1, feats), bf16),
                jax.ShapeDtypeStruct((1, experts), f32),
                jax.ShapeDtypeStruct((1, 1), f32),
            ),
            in_specs=[pl.BlockSpec(memory_space=pltpu.HBM)] * 6,
            out_specs=[pl.BlockSpec(memory_space=pltpu.VMEM)] * 3,
            scratch_shapes=[
                vm((1, 1, feats), bf16),
                vm((1, 1, per_token), jnp.int32),
                vm((1, 1, per_token), jnp.int32),
                vm((2, tiles, 128), bf16),
                vm((2 * tiles, 128), f32),
                vm((2, tiles, 128), bf16),
                vm((2, 1, 128), f32),
                vm((2 * chunk, tiles, 128), bf16),
                vm((2 * chunk, 1, 128), f32),
                vm((SIDE, SIDE, 2 * per_token, 128), f32),
                vm((chunk, tiles, 128), f32),
                vm((128, 128), f32),
                vm((2, 2, SIDE, SIDE, chunk, part), bf16),
                vm((2, part, 4 * hid), bf16),
                vm((2 * hid, 2 * part), bf16),
                vm((2, SIDE, SIDE * chunk, 2 * hid), f32),
                vm((2, SIDE, SIDE * chunk, 2 * hid), f32),
                vm((2, SIDE, SIDE * chunk, 2 * hid), f32),
                vm((2, SIDE, SIDE * chunk, hid), bf16),
                vm((2, SIDE, SIDE * chunk, hid), bf16),
                vm((2, SIDE, SIDE * chunk, hid), f32),
                vm((2, 2, SIDE, SIDE, chunk, part), bf16),
                vm((2, 2, 5, 2, chunk // 2, part), bf16),
                vm((2, 2, 5, 2, chunk, part), bf16),
                vm((2, chunk, tiles, 128), bf16),
                vm((near - 1, 2 * FAR, tiles, 128), bf16),
                vm((2 * FAR, tiles, 128), bf16),
                vm((FAR, 2, tiles, 128), bf16),
                vm((2, tiles, 128), bf16),
                pltpu.SemaphoreType.DMA((N_SEND,)),
                pltpu.SemaphoreType.DMA((N_RECV,)),
                pltpu.SemaphoreType.DMA((5,)),
            ],
            compiler_params=pltpu.CompilerParams(
                collective_id=0, has_side_effects=True, vmem_limit_bytes=63 * 1024 * 1024
            ),
            name="expert_layer",
        )(tokens, routes, gate_num, w_gate, w_up, w_down)
        return out, load.reshape(experts), loss.reshape(())

    column = P(("node", "innode"), "dp", None)
    in_specs = (column, column, column, P(("node", "innode"), None, "dp"), P(("node", "innode"), None, "dp"), column)
    return jax.shard_map(shards, mesh=mesh, in_specs=in_specs, out_specs=(column, P(), P()), check_vma=False)
```

```python
import functools

import jax
import jax.numpy as jnp
from jax import lax
from jax.experimental import pallas as pl
from jax.experimental.pallas import tpu as pltpu
from jax.sharding import PartitionSpec as P

GATE_DEN = 256
MESH = pl.DeviceIdType.MESH
SIDE = 4
N_SEND, N_RECV = 33, 98
FAR = 4


def kernel(
    dims,
    tokens,
    routes,
    gate_num,
    wg,
    wu,
    wd,
    out,
    load_out,
    loss_out,
    tok_in,
    routes_in,
    gates_in,
    tok,
    rows_f,
    pair,
    pair_m,
    x3,
    mz,
    codes,
    spread,
    meta_t,
    xb,
    w1,
    w2,
    pa,
    ps,
    pr,
    h_own,
    h_oth,
    gates_t,
    ob,
    rh,
    rf,
    y3,
    rn,
    ya,
    rz,
    fin,
    ssem,
    rsem,
    lsem,
):
    n_dp, feats, experts, per_token, total_tokens = dims
    ring = 2 * n_dp
    near = ring // FAR
    chunk = ring
    half = chunk // 2
    tiles = feats // 256
    part = feats // 4
    hid = wd.shape[1]
    f32, bf16 = jnp.float32, jnp.bfloat16

    dp = lax.axis_index("dp")
    node = lax.axis_index("node")
    inn = lax.axis_index("innode")
    z = lax.div(node, 2) * n_dp + dp
    core = lax.rem(node, 2)
    other = 1 - core
    py = lax.div(inn, SIDE)
    px = lax.rem(inn, SIDE)

    def device(zz, cc, yy, xx):
        return (lax.rem(zz, n_dp), lax.div(zz, n_dp) * 2 + cc, yy * SIDE + xx)

    def ringz(o):
        return lax.rem(z + (o + ring), ring)

    def side(p, o):
        return lax.rem(p + (o + SIDE), SIDE)

    far = [3 * near // 2, -3 * near // 2, near // 2, -near // 2]
    steps = sorted(range(-near // 2, near // 2), key=abs)
    members = 2 * FAR
    per_chunk = near // 2

    def along(o):
        return device(ringz(o), core, py, px)

    partner = device(z, other, py, px)

    barrier = pltpu.get_barrier_semaphore()
    greet = [along(f) for f in far]
    greet += [along(o) for o in range(near // 2, 0, -1)] + [along(-o) for o in range(near // 2, 0, -1)]
    greet = greet if near > 2 else greet[:2] + [along(1), along(-1)]
    greet += [device(z, core, py, side(px, o)) for o in (2, 1, -1)]
    greet += [device(z, core, side(py, o), px) for o in (2, 1, -1)]
    greet += [partner]
    for target in greet:
        pl.semaphore_signal(barrier, inc=1, device_id=target, device_id_type=MESH)

    def load(src, dst, i):
        copy = pltpu.make_async_copy(src, dst, lsem.at[i])
        copy.start()
        return copy

    def rows_of(c, h):
        return pl.ds(pl.multiple_of(c * (2 * part) + h * part, part), part)

    def lanes_of(c):
        return pl.ds(pl.multiple_of(c * (2 * part), 2 * part), 2 * part)

    small = [load(tokens, tok_in, 0), load(routes, routes_in, 1), load(gate_num, gates_in, 2)]
    for h in range(2):
        load(wg.at[0, rows_of(core, h), :], w1.at[h, :, pl.ds(0, hid)], 3)
        load(wu.at[0, rows_of(core, h), :], w1.at[h, :, pl.ds(hid, hid)], 3)
    load(wd.at[0, :, lanes_of(core)], w2.at[pl.ds(0, hid), :], 4)

    for copy in small:
        copy.wait()
    for i in range(2 * tiles):
        rows_f[pl.ds(i, 1), :] = tok_in[0, :, pl.ds(i * 128, 128)].astype(f32)
    for h in range(2):
        tok[h] = rows_f[pl.ds(h * tiles, tiles), :].astype(bf16)
    pair[core] = tok[core]
    pair_m[core] = jnp.concatenate(
        [
            routes_in[0].astype(f32),
            gates_in[0].astype(f32),
            jnp.zeros((1, 128 - 2 * per_token), f32),
        ],
        axis=1,
    )

    pl.semaphore_wait(barrier, len(greet))

    sends, recvs = {}, {}

    def send(name, src, dst, target, arrival=None, departure=None):
        arrival = name if arrival is None else arrival
        departure = name if departure is None else departure
        pltpu.make_async_remote_copy(
            src_ref=src,
            dst_ref=dst,
            send_sem=ssem.at[sends.setdefault(departure, len(sends))],
            recv_sem=rsem.at[recvs.setdefault(arrival, len(recvs))],
            device_id=target,
            device_id_type=MESH,
        ).start()

    def end_of(like, s_index, r_index):
        return pltpu.make_async_remote_copy(
            src_ref=like,
            dst_ref=like,
            send_sem=ssem.at[s_index],
            recv_sem=rsem.at[r_index],
            device_id=partner,
            device_id_type=MESH,
        )

    def arrived(name, like):
        end_of(like, 0, recvs[name]).wait_recv()

    def departed(name, like):
        end_of(like, sends.pop(name), 0).wait_send()

    send("pair", tok.at[other], pair.at[core], partner)
    send("pairm", pair_m.at[core], pair_m.at[core], partner)
    arrived("pair", tok.at[0])
    for i, f in enumerate(far):
        send("far", pair, x3.at[pl.ds(2 * i, 2)], along(f))
    arrived("pairm", pair_m.at[0])
    for i, f in enumerate(far):
        send("farm", pair_m, mz.at[pl.ds(2 * i, 2)], along(f))

    for h in range(2):
        send("w1", wg.at[0, rows_of(other, h), :], w1.at[h, :, pl.ds(2 * hid, hid)], partner)
        send("w1", wu.at[0, rows_of(other, h), :], w1.at[h, :, pl.ds(3 * hid, hid)], partner)
    send("w2", wd.at[0, :, lanes_of(other)], w2.at[pl.ds(hid, hid), :], partner)

    near_rest = pl.ds(members, (near - 1) * members)
    arrived("far", x3.at[pl.ds(0, members)])
    for g in [*range(1, per_chunk), *range(near - 1, per_chunk - 1, -1)]:
        send("near", x3.at[pl.ds(0, members)], x3.at[pl.ds(g * members, members)], along(steps[g]), ("near", g // per_chunk))
    arrived("farm", mz.at[pl.ds(0, members)])
    for g in range(1, near):
        send("nearm", mz.at[pl.ds(0, members)], mz.at[pl.ds(g * members, members)], along(steps[g]))

    def place(h, da, db):
        return (side(py, db), side(px, da)) if h == 0 else (side(py, da), side(px, db))

    def xy_device(h, da, db):
        yy, xx = place(h, da, db)
        return device(z, core, yy, xx)

    def block(ref, q, h, da, db, rows=None):
        yy, xx = place(h, da, db)
        return ref.at[q, h, yy, xx] if rows is None else ref.at[q, h, yy, xx, rows]

    low, high = pl.ds(0, half), pl.ds(half, half)

    def ag_own(q):
        for h in range(2):
            for d in (1, -1):
                src = block(xb, q, h, 0, 0)
                send(("p1", q, h), src, src, xy_device(h, d, 0), None, ("full", q, h))

    def ag_middle(q):
        for h in range(2):
            ag_second(q, h, 0)

    def ag_second(q, h, a):
        src = block(xb, q, h, a, 0)
        for d in (1, -1):
            send(("p2", q, h, a), src, src, xy_device(h, 0, d), None, ("full", q, h))

    def ag_first_forward(q):
        for h in range(2):
            arrived(("p1", q, h), rf.at[q, h, 0])
            for d in (1, -1):
                src = block(xb, q, h, -d, 0, low if d == 1 else high)
                send(("p1f", q, h), src, src, xy_device(h, d, 0), None, ("half", q, h))

    def ag_sides(q):
        for d in (1, -1):
            for h in range(2):
                ag_second(q, h, d)

    def ag_second_forward(q, a):
        for h in range(2):
            arrived(("p2", q, h, a), rf.at[q, h, 0])
            for d in (1, -1):
                src = block(xb, q, h, a, -d, low if d == 1 else high)
                send(("p2f", q, h), src, src, xy_device(h, 0, d), None, ("half", q, h))

    def ag_opposite(q):
        for h in range(2):
            arrived(("p1f", q, h), block(xb, q, h, 2, 0))
            ag_second(q, h, 2)

    def ag_finish(q):
        for h in range(2):
            arrived(("p2f", q, h), rh.at[q, h, pl.ds(0, SIDE)])

    def spread_in(q):
        first = members if q == 0 else 0
        arrived(("near", q), x3.at[pl.ds(q * chunk + first, chunk - first)])
        spread[...] = x3[pl.ds(q * chunk, chunk)].astype(f32)
        per = part // 128
        for h in range(2):
            for i in range(per):
                xb[q, h, py, px, :, pl.ds(i * 128, 128)] = spread[:, h * per + i, :].astype(bf16)

    turn = (2, 1, -1, 0)

    def project(q):
        rows = SIDE * SIDE * chunk
        acc = jnp.dot(xb[q, 0].reshape(rows, part), w1[0], preferred_element_type=f32)
        acc = acc + jnp.dot(xb[q, 1].reshape(rows, part), w1[1], preferred_element_type=f32)
        ps[q] = acc[:, 2 * hid : 4 * hid].reshape(SIDE, SIDE * chunk, 2 * hid)
        for t in turn:
            yy = side(py, t)
            send(("ps", q, t), ps.at[q, yy], pr.at[q, yy], partner, None, ("ps", q))
        pa[q] = acc[:, 0 : 2 * hid].reshape(SIDE, SIDE * chunk, 2 * hid)

    def activate(q):
        for t in turn:
            yy = side(py, t)
            arrived(("ps", q, t), ps.at[q, 0])
            pre = pa[q, yy] + pr[q, yy]
            gate, up = pre[:, 0:hid], pre[:, hid : 2 * hid]
            hidden = gate / (1.0 + jnp.exp(-gate)) * up
            for xx in range(SIDE):
                column = gates_t[q, yy, pl.ds(xx * chunk, chunk), :]
                piece = hidden[xx * chunk : (xx + 1) * chunk] * column
                h_own[q, yy, pl.ds(xx * chunk, chunk), :] = piece.astype(bf16)
            send(("h", q, t), h_own.at[q, yy], h_oth.at[q, yy], partner, None, ("h", q))

    index_of = {0: 0, 1: 1, -1: 2, 2: 3}

    def expand(q):
        for t in turn:
            yy = side(py, t)
            arrived(("h", q, t), h_own.at[q, 0])
            hidden = jnp.concatenate([h_own[q, yy], h_oth[q, yy]], axis=1)
            for h in range(2):
                val = jnp.dot(hidden, w2[:, h * part : (h + 1) * part], preferred_element_type=f32)
                ob[q, h, yy] = val.astype(bf16).reshape(SIDE, chunk, part)
            if t == 2:
                for a in turn:
                    rs_far(q, 0, a)
            rs_far(q, 1, t)

    def rs_far(q, h, a):
        for d in (1, -1):
            src = block(ob, q, h, a, 2, low if d == 1 else high)
            dst = rh.at[q, h, index_of[a], (1 - d) // 2]
            send(("r1", q, h, a), src, dst, xy_device(h, 0, d), None, ("rhalf", q, h))

    def add_half(q, h, da, db, rows, src):
        yy, xx = place(h, da, db)
        ob[q, h, yy, xx, rows] = ob[q, h, yy, xx, rows] + src

    def rs_side(q, a):
        for h in range(2):
            i = index_of[a]
            arrived(("r1", q, h, a), rh.at[q, h, i])
            for d in (1, -1):
                add_half(q, h, a, d, low if d == 1 else high, rh[q, h, i, (1 - d) // 2])
                dst = rf.at[q, h, i, (1 - d) // 2]
                send(("r2", q, h, a), block(ob, q, h, a, d), dst, xy_device(h, 0, d), None, ("rfull", q, h))

    def rs_take(q, h, a):
        i = index_of[a]
        arrived(("r2", q, h, a), rf.at[q, h, i])
        yy, xx = place(h, a, 0)
        return ob[q, h, yy, xx].astype(f32) + rf[q, h, i, 0].astype(f32) + rf[q, h, i, 1].astype(f32)

    def rs_second_far(q):
        for h in range(2):
            yy, xx = place(h, 2, 0)
            ob[q, h, yy, xx] = rs_take(q, h, 2).astype(bf16)
            for d in (1, -1):
                src = block(ob, q, h, 2, 0, low if d == 1 else high)
                dst = rh.at[q, h, 4, (1 - d) // 2]
                send(("r3", q, h), src, dst, xy_device(h, d, 0), None, ("rhalf", q, h))

    def rs_second_side(q):
        for h in range(2):
            for d in (1, -1):
                yy, xx = place(h, d, 0)
                ob[q, h, yy, xx] = rs_take(q, h, d).astype(bf16)
        for h in range(2):
            arrived(("r3", q, h), rh.at[q, h, 4])
            for d in (1, -1):
                add_half(q, h, d, 0, low if d == 1 else high, rh[q, h, 4, (1 - d) // 2])
                dst = rf.at[q, h, 4, (1 - d) // 2]
                send(("r4", q, h), block(ob, q, h, d, 0), dst, xy_device(h, d, 0), None, ("rfull", q, h))

    def rs_last(q):
        per = part // 128
        for h in range(2):
            total = rs_take(q, h, 0)
            arrived(("r4", q, h), rf.at[q, h, 4])
            total = total + rf[q, h, 4, 0].astype(f32) + rf[q, h, 4, 1].astype(f32)
            for i in range(per):
                spread[:, h * per + i, :] = total[:, i * 128 : (i + 1) * 128]
        y3[q] = spread[...].astype(bf16)
        for g in reversed(range(q * per_chunk, (q + 1) * per_chunk)):
            if g:
                src = y3.at[q, pl.ds((g - q * per_chunk) * members, members)]
                send("zn", src, rn.at[g - 1], along(-steps[g]))

    def statistics():
        rows_e = lax.broadcasted_iota(jnp.int32, (experts, 128), 0).astype(f32)

        def body(i, carry):
            counts, share_sums = carry
            table = codes[lax.div(i, SIDE), lax.rem(i, SIDE)]
            route, numer = table[0:per_token], table[per_token : 2 * per_token]
            numer = jnp.where(route >= 0, numer, 0.0)
            total = jnp.sum(numer, axis=0, keepdims=True)
            share = numer / jnp.where(total > 0, total, 1.0)
            for k in range(per_token):
                hit = rows_e == route[k : k + 1]
                counts = counts + jnp.where(hit, 1.0, 0.0)
                share_sums = share_sums + jnp.where(hit, share[k : k + 1], 0.0)
            return counts, share_sums

        zero = jnp.zeros((experts, 128), f32)
        counts, share_sums = lax.fori_loop(0, SIDE * SIDE, body, (zero, zero))
        load_col = jnp.sum(counts, axis=1, keepdims=True) * (experts / (per_token * total_tokens))
        mean_col = jnp.sum(share_sums, axis=1, keepdims=True) / total_tokens
        meta_t[pl.ds(0, experts), :] = jnp.broadcast_to(load_col, (experts, 128))
        load_out[...] = jnp.transpose(meta_t[...])[0:1, 0:experts]
        loss_out[...] = jnp.sum(load_col * mean_col, axis=0, keepdims=True)

    def codes_own():
        arrived("nearm", mz.at[near_rest])
        meta_t[...] = jnp.full_like(meta_t, -1.0)
        meta_t[pl.ds(0, 2 * chunk), :] = mz[:, 0, :]
        codes[py, px] = jnp.transpose(meta_t[...])[0 : 2 * per_token]
        for o in (2, 1, -1):
            src = codes.at[py, px]
            send("mx", src, src, device(z, core, py, side(px, o)))

    def codes_row():
        arrived("mx", codes.at[0, pl.ds(0, 3)])
        for o in (2, 1, -1):
            src = codes.at[py]
            send("my", src, src, device(z, core, side(py, o), px))

    def gates():
        arrived("my", codes.at[pl.ds(0, 3)])
        expert = (node * (SIDE * SIDE) + inn).astype(f32)
        meta_t[...] = jnp.zeros_like(meta_t)
        for yy in range(SIDE):
            for xx in range(SIDE):
                route, numer = codes[yy, xx, 0:per_token], codes[yy, xx, per_token : 2 * per_token]
                meta_t[pl.ds(yy * SIDE + xx, 1), :] = jnp.sum(
                    jnp.where(route == expert, numer, 0.0), axis=0, keepdims=True
                ) * (1.0 / GATE_DEN)
        columns = jnp.transpose(meta_t[...])
        for q in range(2):
            for yy in range(SIDE):
                for xx in range(SIDE):
                    i = yy * SIDE + xx
                    column = columns[q * chunk : (q + 1) * chunk, i : i + 1]
                    gates_t[q, yy, pl.ds(xx * chunk, chunk), :] = jnp.broadcast_to(column, (chunk, hid))

    spread_in(0)
    ag_own(0)
    ag_middle(0)
    spread_in(1)
    ag_own(1)
    codes_own()
    ag_first_forward(0)
    ag_sides(0)
    ag_first_forward(1)
    ag_middle(1)
    ag_opposite(0)
    ag_opposite(1)
    ag_second_forward(0, 0)
    ag_second_forward(0, 1)
    ag_second_forward(0, -1)
    ag_sides(1)
    codes_row()
    ag_second_forward(0, 2)
    ag_second_forward(1, 0)
    ag_second_forward(1, 2)
    pltpu.make_async_copy(w1.at[:, :, pl.ds(0, 2 * hid)], w1.at[:, :, pl.ds(0, 2 * hid)], lsem.at[3]).wait()
    pltpu.make_async_copy(w2.at[pl.ds(0, hid), :], w2.at[pl.ds(0, hid), :], lsem.at[4]).wait()
    arrived("w1", w1.at[:, :, pl.ds(2 * hid, 2 * hid)])
    arrived("w2", w2.at[pl.ds(hid, hid), :])
    ag_finish(0)
    project(0)
    ag_second_forward(1, 1)
    ag_second_forward(1, -1)
    gates()
    activate(0)
    expand(0)
    ag_finish(1)
    project(1)
    rs_side(0, 2)
    rs_side(0, 1)
    rs_side(0, -1)
    activate(1)
    rs_side(0, 0)
    rs_second_far(0)
    expand(1)
    rs_second_side(0)
    rs_side(1, 2)
    rs_side(1, 1)
    rs_side(1, -1)
    rs_second_far(1)
    rs_side(1, 0)
    rs_last(0)
    rs_second_side(1)
    rs_last(1)

    arrived("zn", rn)
    total = y3[0, pl.ds(0, members)].astype(f32)
    for g in range(near - 1):
        total = total + rn[g].astype(f32)
    ya[...] = total.astype(bf16)
    for i, f in enumerate(far):
        send("zf", ya.at[pl.ds(2 * i, 2)], rz.at[i], along(-f))
    statistics()
    for q in range(2):
        for h in range(2):
            departed(("full", q, h), rf.at[q, h])
            departed(("half", q, h), rh.at[q, h])
            departed(("rfull", q, h), rf.at[q, h])
            departed(("rhalf", q, h), rh.at[q, h])
        departed(("ps", q), ps.at[q])
        departed(("h", q), h_own.at[q])
    departed("pair", tok.at[0])
    departed("pairm", pair_m.at[0])
    departed("far", x3.at[pl.ds(0, members)])
    departed("farm", mz.at[pl.ds(0, members)])
    departed("near", x3.at[near_rest])
    departed("nearm", mz.at[near_rest])
    departed("w1", w1.at[:, :, pl.ds(2 * hid, 2 * hid)])
    departed("w2", w2.at[pl.ds(hid, hid), :])
    departed("mx", codes.at[0, pl.ds(0, 3)])
    departed("my", codes.at[pl.ds(0, 3)])
    departed("zn", rn)
    departed("zf", rz)
    arrived("zf", rz)

    def gathered(c):
        return rz[0, c].astype(f32) + rz[1, c].astype(f32) + rz[2, c].astype(f32) + rz[3, c].astype(f32)

    fin[other] = gathered(other).astype(bf16)
    send("fin", fin.at[other], fin.at[other], partner)
    rows_f[pl.ds(pl.multiple_of(core * tiles, tiles), tiles), :] = gathered(core)
    arrived("fin", fin.at[0])
    rows_f[pl.ds(pl.multiple_of(other * tiles, tiles), tiles), :] = fin[core].astype(f32)
    for i in range(2 * tiles):
        out[0, :, pl.ds(i * 128, 128)] = rows_f[pl.ds(i, 1), :].astype(bf16)
    departed("fin", fin.at[0])


def solution(mesh):
    n_dp = mesh.shape["dp"]

    def shards(tokens, routes, gate_num, w_gate, w_up, w_down):
        feats = tokens.shape[2]
        per_token = routes.shape[2]
        hid = w_down.shape[1]
        experts = mesh.shape["node"] * mesh.shape["innode"]
        ring = 2 * n_dp
        chunk, near = ring, ring // FAR
        tiles, part = feats // 256, feats // 4
        dims = (n_dp, feats, experts, per_token, n_dp * experts)
        bf16, f32 = jnp.bfloat16, jnp.float32
        vm = pltpu.VMEM
        out, load, loss = pl.pallas_call(
            functools.partial(kernel, dims),
            out_shape=(
                jax.ShapeDtypeStruct((1, 1, feats), bf16),
                jax.ShapeDtypeStruct((1, experts), f32),
                jax.ShapeDtypeStruct((1, 1), f32),
            ),
            in_specs=[pl.BlockSpec(memory_space=pltpu.HBM)] * 6,
            out_specs=[pl.BlockSpec(memory_space=pltpu.VMEM)] * 3,
            scratch_shapes=[
                vm((1, 1, feats), bf16),
                vm((1, 1, per_token), jnp.int32),
                vm((1, 1, per_token), jnp.int32),
                vm((2, tiles, 128), bf16),
                vm((2 * tiles, 128), f32),
                vm((2, tiles, 128), bf16),
                vm((2, 1, 128), f32),
                vm((2 * chunk, tiles, 128), bf16),
                vm((2 * chunk, 1, 128), f32),
                vm((SIDE, SIDE, 2 * per_token, 128), f32),
                vm((chunk, tiles, 128), f32),
                vm((128, 128), f32),
                vm((2, 2, SIDE, SIDE, chunk, part), bf16),
                vm((2, part, 4 * hid), bf16),
                vm((2 * hid, 2 * part), bf16),
                vm((2, SIDE, SIDE * chunk, 2 * hid), f32),
                vm((2, SIDE, SIDE * chunk, 2 * hid), f32),
                vm((2, SIDE, SIDE * chunk, 2 * hid), f32),
                vm((2, SIDE, SIDE * chunk, hid), bf16),
                vm((2, SIDE, SIDE * chunk, hid), bf16),
                vm((2, SIDE, SIDE * chunk, hid), f32),
                vm((2, 2, SIDE, SIDE, chunk, part), bf16),
                vm((2, 2, 5, 2, chunk // 2, part), bf16),
                vm((2, 2, 5, 2, chunk, part), bf16),
                vm((2, chunk, tiles, 128), bf16),
                vm((near - 1, 2 * FAR, tiles, 128), bf16),
                vm((2 * FAR, tiles, 128), bf16),
                vm((FAR, 2, tiles, 128), bf16),
                vm((2, tiles, 128), bf16),
                pltpu.SemaphoreType.DMA((N_SEND,)),
                pltpu.SemaphoreType.DMA((N_RECV,)),
                pltpu.SemaphoreType.DMA((5,)),
            ],
            compiler_params=pltpu.CompilerParams(
                collective_id=0, has_side_effects=True, vmem_limit_bytes=63 * 1024 * 1024
            ),
            name="expert_layer",
        )(tokens, routes, gate_num, w_gate, w_up, w_down)
        return out, load.reshape(experts), loss.reshape(())

    column = P(("node", "innode"), "dp", None)
    in_specs = (column, column, column, P(("node", "innode"), None, "dp"), P(("node", "innode"), None, "dp"), column)
    return jax.shard_map(shards, mesh=mesh, in_specs=in_specs, out_specs=(column, P(), P()), check_vma=False)
```
